32 devices in a mesh: rng: 4 (over y, x), az: 8 (over z, core).
Axes of the slice: x: 2, y: 2, z: 4, core: 2. Of those that a mesh axis runs over, the one named last changes fastest.
Arguments:
- echoes: bfloat16 [8, 2, 64, 6144], P('az', None, None, 'rng'), may hold values from -6 to 6
- owner_map: int32 [8], replicated, may hold values from 0 to 7, as said below
- band_start: int32 [24, 8, 8], P('rng', 'az'), may hold values from 0 to 1536, as said below
- interp: bfloat16 [8, 8, 3072, 256], P(None, 'az', 'rng'), may hold values from -0.375 to 0.375
- steer_phase: float32 [8, 64, 8192], P(None, None, 'az'), may hold values from -3.140625 to 3.140625
Outputs:
- focused_image: bfloat16 [3072, 2, 8192], P('rng', None, 'az')
The draws below stay inside these ranges and needn't reach their ends.
Inputs may be any that keep to these rules, and one draw needn't show every extreme that they name: `owner_map`: the pings' slots are distinct. band_start[g, j, p] lies within 128 of (g mod 6) * 256 + 128.
All inputs are finite; a program needn't handle non-finite values.
Results may differ from the reference program's by a relative error of at most 0.01.
The reference program's roundings to bfloat16 on the way count: a program that leaves them out, or rounds other values in their place, can miss the bound.
Values may be sent and summed in bfloat16 or wider, within the bound.
A program may use at most 128 MiB of HBM per device.

```python
import jax
import jax.numpy as jnp
from jax import lax

H = 64
PINGS = 8
BLK = 128
GUARD = 128
NBLK = 6
A_DEV = 1024
BAND = 256
S_DEV = 1536
NR = 3072
NA = 8192
NS = 6144
NBT = 24
N_RNG = 4
N_AZ = 8


def draw_owner_map(key, part):
    slots = NA // A_DEV
    first_key = jax.random.fold_in(key, 11)
    second_key = jax.random.fold_in(key, 12)
    inner = 1 + jax.random.permutation(first_key, slots - 2)[:PINGS - 2]
    values = jnp.concatenate([jnp.array([0, slots - 1], jnp.int32), inner.astype(jnp.int32)])
    order = jax.random.permutation(second_key, PINGS)
    return values[order].astype(jnp.int32)


def draw_band_start(key, part):
    slots = NA // A_DEV
    shift_key = jax.random.fold_in(key, 21)
    delay = jax.random.randint(shift_key, (NBT, slots, PINGS), -GUARD, GUARD + 1).astype(jnp.int32)
    delay = delay.at[0, 0, 0].set(-GUARD)
    delay = delay.at[NBT - 1, slots - 1, PINGS - 1].set(GUARD)
    nominal = jnp.arange(NBT).astype(jnp.int32) % NBLK * BAND + GUARD
    return (nominal[:, None, None] + delay).astype(jnp.int32)


def steps_of(rng, shape, pieces, smallest, top_value):
    factor_of, own = 1.0, jax.random.fold_in(rng, 6)
    for dim, blocks in pieces:
        steps = jnp.exp(jax.random.uniform(jax.random.fold_in(own, dim), (blocks,), jnp.float32, smallest / len(pieces), top_value / len(pieces)))
        factor_of = factor_of * jnp.repeat(steps, shape[dim] // blocks).reshape([-1 if axis == dim else 1 for axis in range(len(shape))])
    return factor_of


def centred(stream_key, dims, scale, most, pieces=(), kind=jnp.bfloat16):
    entries = jax.random.normal(stream_key, dims, jnp.float32) * scale
    if len(pieces) > 0:
        entries = steps_of(stream_key, dims, pieces, -0.22, 0.18) * entries
    return jnp.clip(entries, min=-most, max=most).astype(kind)


def setup_inputs(seed: int = 0) -> dict:
    keys = jax.random.split(jax.random.key(seed), 6)
    return {
        "echoes": centred(keys[0], (N_AZ, 2, H, NS), 1.0, 6.0, ((0, 8), (3, 4))),
        "owner_map": draw_owner_map(jax.random.fold_in(keys[5], 71), 0),
        "band_start": draw_band_start(jax.random.fold_in(keys[5], 71), 0),
        "interp": centred(keys[3], (PINGS, N_AZ, NR, BAND), BAND ** -0.5, 0.375, ((1, 8), (2, 4))),
        "steer_phase": jnp.clip(jax.random.uniform(keys[4], (PINGS, H, NA), jnp.float32, -3.140625, 3.140625), -3.140625, 3.140625),
    }


def autofocus_pass(image):
    blocks = image.reshape(N_RNG, NR // N_RNG, 2, NA)

    def sums(block):
        real_part = block[:, 0].astype(jnp.float32)
        imag_part = block[:, 1].astype(jnp.float32)
        cross = lax.optimization_barrier(jnp.sum(real_part[:, :-1] * imag_part[:, 1:] - imag_part[:, :-1] * real_part[:, 1:], axis=0))
        cross = jnp.concatenate([cross, jnp.zeros((1,), jnp.float32)])
        power = lax.optimization_barrier(jnp.sum(real_part * real_part + imag_part * imag_part, axis=0))
        return (cross, power)
    cross, power = lax.map(sums, blocks)
    cross = lax.optimization_barrier(jnp.sum(cross, axis=0))
    power = lax.optimization_barrier(jnp.sum(power, axis=0))
    slope = cross / (power + 1e-06)
    phase = jnp.cumsum(slope) - slope
    cosine = jnp.cos(phase)
    sine = jnp.sin(phase)

    def correct(block):
        real_part = block[:, 0].astype(jnp.float32)
        imag_part = block[:, 1].astype(jnp.float32)
        return jnp.stack([real_part * cosine + imag_part * sine, imag_part * cosine - real_part * sine], axis=1).astype(jnp.bfloat16)
    return lax.map(correct, blocks).reshape(NR, 2, NA)

def reference(echoes, owner_map, band_start, interp, steer_phase):
    padded = jnp.pad(echoes, ((0, 0), (0, 0), (0, 0), (GUARD, GUARD)))
    windows = padded[owner_map]
    scale = 1.0 / jnp.sqrt(jnp.float32(PINGS * H))
    tile_of_block = (jnp.arange(NBT) // NBLK).astype(jnp.int32)

    def one_tile(column):
        starts = lax.dynamic_slice_in_dim(band_start, column, 1, 1)[:, 0, :]
        offsets = tile_of_block[:, None] * S_DEV + starts

        def cut(window, start):
            return lax.dynamic_slice_in_dim(window, start, BAND, 2)
        slabs = jax.vmap(jax.vmap(cut, (0, 0)), (None, 0))(windows, offsets)
        kernels = lax.dynamic_slice_in_dim(interp, column, 1, 1)[:, 0].reshape(PINGS, NBT, BLK, BAND)
        focused = jnp.einsum('pgik,gpchk->gipch', kernels.astype(jnp.float32), slabs.astype(jnp.float32))
        focused = focused.astype(jnp.bfloat16).reshape(NR, PINGS * 2 * H)
        phases = lax.dynamic_slice_in_dim(steer_phase, column * A_DEV, A_DEV, 2)
        steer_re = (jnp.cos(phases) * scale).astype(jnp.bfloat16)
        steer_im = (jnp.sin(phases) * scale).astype(jnp.bfloat16)
        upper = jnp.stack([steer_re, steer_im], axis=2)
        lower = jnp.stack([-steer_im, steer_re], axis=2)
        steering = jnp.stack([upper, lower], axis=1).reshape(PINGS * 2 * H, 2 * A_DEV)
        return jnp.dot(focused, steering, preferred_element_type=jnp.float32).astype(jnp.bfloat16)
    tiles = lax.map(one_tile, jnp.arange(N_AZ).astype(jnp.int32))
    image0 = jnp.transpose(tiles.reshape(N_AZ, NR, 2, A_DEV), (1, 2, 0, 3)).reshape(NR, 2, NA)
    image1 = autofocus_pass(image0)
    return autofocus_pass(image1)
```

```python
import functools

import jax
import jax.numpy as jnp
from jax import lax
from jax.experimental import pallas as pl
from jax.experimental.pallas import tpu as pltpu
from jax.sharding import PartitionSpec as P

GUARD = 128
MESH = pl.DeviceIdType.MESH
RIGHT, LEFT, SIBLING, LOW, HIGH = range(5)


def sine_cosine(x):
    turns = jnp.floor(x * 0.6366197723675814 + 0.5)
    r = x - turns * 1.5703125
    r = r - turns * 4.837512969970703e-4
    r = r - turns * 7.549789948768648e-8
    quadrant = turns.astype(jnp.int32)
    r2 = r * r
    s = r + r * r2 * (-1 / 6 + r2 * (1 / 120 + r2 * (-1 / 5040 + r2 * (1 / 362880))))
    c = 1.0 + r2 * (-0.5 + r2 * (1 / 24 + r2 * (-1 / 720 + r2 * (1 / 40320))))
    odd = (quadrant & 1) == 1
    sine = jnp.where(odd, c, s)
    cosine = jnp.where(odd, s, c)
    sine = jnp.where((quadrant & 2) == 2, -sine, sine)
    cosine = jnp.where(((quadrant + 1) & 2) == 2, -cosine, cosine)
    return sine, cosine


def transposed_dot(a, b):
    return lax.dot_general(a, b, (((1,), (1,)), ((), ())), preferred_element_type=jnp.float32)


def kernel(
    n_rng, n_az, pings, blocks,
    ping_of, used, shift, echo, interp, phase,
    out_re, out_im,
    window, interp_v, phase_v, shifted, steer, focus, image, column, sums, totals,
    load_sem, send_sem, recv_sem, column_sem, sum_send, sum_recv, total_send, total_recv,
):
    rng, az = lax.axis_index("rng"), lax.axis_index("az")
    chips = n_az // 2
    chip, core = az // 2, az % 2
    width = echo.shape[1]
    rows = echo.shape[0]
    half = rows // 2
    cells = interp.shape[1]
    band = interp.shape[2]
    azimuths = phase.shape[2]
    block = cells // blocks
    step = width // blocks
    span = band + 2 * GUARD
    scale = 1.0 / (pings * half) ** 0.5

    barrier = pltpu.get_barrier_semaphore()
    for turn in range(1, n_rng):
        pl.semaphore_signal(barrier, inc=1, device_id={"rng": lax.rem(rng + turn, n_rng)}, device_id_type=MESH)
    for turn in range(1, n_az):
        pl.semaphore_signal(barrier, inc=1, device_id={"az": lax.rem(az + turn, n_az)}, device_id_type=MESH)
    pl.semaphore_wait(barrier, n_rng + n_az - 2)

    def inner(slot):
        return window.at[slot, :, pl.ds(GUARD, width)]

    def push(src, dst, sent, got, target):
        return pltpu.make_async_remote_copy(
            src_ref=src, dst_ref=dst, send_sem=sent, recv_sem=got, device_id=target, device_id_type=MESH
        )

    def along(src, slot, kind):
        target = {RIGHT: az + 2, LEFT: az - 2, SIBLING: az + 1 - 2 * core}[kind]
        return push(src, inner(slot), send_sem.at[kind, slot], recv_sem.at[0, slot], {"az": target})

    def edge_low(src, slot):
        return push(
            src.at[:, pl.ds(width - GUARD, GUARD)], window.at[slot, :, pl.ds(0, GUARD)],
            send_sem.at[LOW, slot], recv_sem.at[1, slot], {"rng": rng + 1},
        )

    def edge_high(src, slot):
        return push(
            src.at[:, pl.ds(0, GUARD)], window.at[slot, :, pl.ds(GUARD + width, GUARD)],
            send_sem.at[HIGH, slot], recv_sem.at[2, slot], {"rng": rng - 1},
        )

    def send_edges(src, slot):
        @pl.when(rng + 1 < n_rng)
        def _():
            edge_low(src, slot).start()

        @pl.when(rng > 0)
        def _():
            edge_high(src, slot).start()

    def wait_edges(slot):
        @pl.when(rng > 0)
        def _():
            edge_low(inner(slot), slot).wait_recv()

        @pl.when(rng + 1 < n_rng)
        def _():
            edge_high(inner(slot), slot).wait_recv()

    @pl.when(chip + 1 < chips)
    def _():
        along(echo, az, RIGHT).start()

    @pl.when(chip > 0)
    def _():
        along(echo, az, LEFT).start()

    along(echo, az, SIBLING).start()
    send_edges(echo, az)
    own_copy = pltpu.make_async_copy(echo, inner(az), load_sem.at[0])
    own_copy.start()
    interp_copy = pltpu.make_async_copy(interp, interp_v, load_sem.at[1])
    interp_copy.start()
    phase_copy = pltpu.make_async_copy(phase, phase_v, load_sem.at[2])
    phase_copy.start()

    @pl.when(rng == 0)
    def _():
        window[:, :, 0:GUARD] = jnp.zeros((n_az, rows, GUARD), window.dtype)

    @pl.when(rng == n_rng - 1)
    def _():
        window[:, :, GUARD + width:] = jnp.zeros((n_az, rows, GUARD), window.dtype)

    def prepare(where):
        for side in range(2):
            slot = 2 * where + side
            ping = ping_of[slot]

            def one_block(g, carry):
                part = interp_v[ping, pl.ds(g * block, block), :].astype(jnp.float32)
                if n_az != pings:
                    part = part * used[slot]
                part = jnp.concatenate([part, jnp.zeros((block, span - band), jnp.float32)], axis=1)
                part = pltpu.roll(part, shift[g, ping], 1)
                shifted[slot, pl.ds(g * block, block), :] = part.astype(jnp.bfloat16)
                return carry

            lax.fori_loop(0, blocks, one_block, 0)

            def one_rows(k, carry):
                sine, cosine = sine_cosine(phase_v[ping, pl.ds(k * 16, 16), :])
                sine, cosine = sine * scale, cosine * scale
                top = pl.ds(side * rows + k * 16, 16)
                low = pl.ds(side * rows + half + k * 16, 16)
                steer[where, top, 0:azimuths] = cosine.astype(jnp.bfloat16)
                steer[where, top, azimuths:] = sine.astype(jnp.bfloat16)
                steer[where, low, 0:azimuths] = (-sine).astype(jnp.bfloat16)
                steer[where, low, azimuths:] = cosine.astype(jnp.bfloat16)
                return carry

            lax.fori_loop(0, half // 16, one_rows, 0)

    def compute(where, first):
        for side in range(2):
            slot = 2 * where + side
            for g in range(blocks):
                got = transposed_dot(
                    shifted[slot, pl.ds(g * block, block), :], window[slot, :, pl.ds(g * step, span)]
                )
                focus[pl.ds(g * block, block), side * rows:(side + 1) * rows] = got.astype(jnp.bfloat16)

        def one_rows(k, carry):
            at = pl.ds(k * block, block)
            for part in range(2 * azimuths // 512):
                columns = pl.ds(part * 512, 512)
                got = jnp.dot(focus[at, :], steer[where, :, columns], preferred_element_type=jnp.float32)
                if first:
                    image[at, columns] = got
                else:
                    image[at, columns] = image[at, columns] + got
            return carry

        lax.fori_loop(0, blocks, one_rows, 0)

    interp_copy.wait()
    phase_copy.wait()
    prepare(chip)
    own_copy.wait()
    sibling = 2 * chip + 1 - core
    along(inner(sibling), sibling, SIBLING).wait_recv()
    send_edges(inner(sibling), sibling)
    wait_edges(az)
    wait_edges(sibling)
    compute(chip, True)

    def at_distance(distance, carry):
        sides = ((chip - distance, chip - distance >= 0, RIGHT), (chip + distance, chip + distance < chips, LEFT))
        for where, there, _ in sides:
            @pl.when(there)
            def _():
                prepare(where)

        for where, there, onward in sides:
            @pl.when(there)
            def _():
                slot = 2 * where + core
                along(inner(slot), slot, onward).wait_recv()
                more = chip + 1 < chips if onward == RIGHT else chip > 0

                @pl.when(more)
                def _():
                    along(inner(slot), slot, onward).start()

                along(inner(slot), slot, SIBLING).start()
                send_edges(inner(slot), slot)

        for where, there, _ in sides:
            @pl.when(there)
            def _():
                slot = 2 * where + 1 - core
                along(inner(slot), slot, SIBLING).wait_recv()
                send_edges(inner(slot), slot)

        for where, there, _ in sides:
            @pl.when(there)
            def _():
                wait_edges(2 * where)
                wait_edges(2 * where + 1)
                compute(where, False)

        return carry

    lax.fori_loop(1, chips, at_distance, 0)

    def one_group(k, carry):
        cross_re, cross_im, power = carry
        at = pl.ds(k * 16, 16)
        re16 = image[at, 0:azimuths].astype(jnp.bfloat16)
        im16 = image[at, azimuths:].astype(jnp.bfloat16)
        out_re[at, :] = re16
        out_im[at, :] = im16
        re, im = re16.astype(jnp.float32), im16.astype(jnp.float32)
        re_next = pltpu.roll(re, azimuths - 1, 1)
        im_next = pltpu.roll(im, azimuths - 1, 1)

        def fold(x):
            return x[0:8] + x[8:16]

        return (
            cross_re + fold(re * re_next + im * im_next),
            cross_im + fold(re * im_next - im * re_next),
            power + fold(re * re + im * im),
        )

    zero = jnp.zeros((8, azimuths), jnp.float32)
    cross_re, cross_im, power = lax.fori_loop(0, cells // 16, one_group, (zero, zero, zero))

    row16 = lax.broadcasted_iota(jnp.int32, (16, 128), 0)
    lane16 = lax.broadcasted_iota(jnp.int32, (16, 128), 1)

    def pick(row, lane):
        return jnp.where((row16 == row) & (lane16 == lane), 1.0, 0.0).astype(jnp.bfloat16)

    head = transposed_dot(pick(0, 0), out_re[:, 0:128]) + transposed_dot(pick(1, 0), out_im[:, 0:128])
    column[0] = head[0:8]
    send_column = push(
        column.at[0], column.at[1], column_sem.at[0], column_sem.at[1], {"az": lax.rem(az + n_az - 1, n_az)}
    )
    send_column.start()
    tail_re = transposed_dot(pick(0, 127), out_re[:, azimuths - 128:])
    tail_im = transposed_dot(pick(0, 127), out_im[:, azimuths - 128:])
    send_column.wait_recv()
    next_re, next_im = column[1, 0:1, :], column[1, 1:2, :]
    last_re, last_im = tail_re[0:1], tail_im[0:1]
    inside = jnp.where(az == n_az - 1, 0.0, 1.0)
    edge_re = jnp.sum(last_re * next_re + last_im * next_im, axis=1, keepdims=True) * inside
    edge_im = jnp.sum(last_re * next_im - last_im * next_re, axis=1, keepdims=True) * inside

    lane = lax.broadcasted_iota(jnp.int32, (8, azimuths), 1)
    row = lax.broadcasted_iota(jnp.int32, (8, azimuths), 0)
    at_end = lane == azimuths - 1
    cross_re = jnp.where(at_end, edge_re, jnp.sum(cross_re, axis=0, keepdims=True))
    cross_im = jnp.where(at_end, edge_im, jnp.sum(cross_im, axis=0, keepdims=True))
    power = jnp.sum(power, axis=0, keepdims=True)
    sums[rng] = jnp.where(row == 0, cross_re, jnp.where(row == 1, cross_im, power))

    def send_sums(turn):
        peer = lax.rem(rng + turn, n_rng)
        return push(sums.at[rng], sums.at[rng], sum_send.at[turn], sum_recv.at[rng], {"rng": peer})

    def take_sums(turn):
        peer = lax.rem(rng + turn, n_rng)
        return push(sums.at[peer], sums.at[peer], sum_send.at[turn], sum_recv.at[peer], {"rng": peer})

    for turn in range(1, n_rng):
        send_sums(turn).start()
    for turn in range(1, n_rng):
        take_sums(turn).wait_recv()
    total = sums[0]
    for turn in range(1, n_rng):
        total = total + sums[turn]
    cross_re, cross_im, power = total[0:1], total[1:2], total[2:3] + 1e-06
    slope = cross_im / power
    slope = slope + (cross_im * jnp.cos(slope) - cross_re * jnp.sin(slope)) / power
    slope = jnp.broadcast_to(slope, (8, azimuths))
    running = slope
    reach = 1
    while reach < azimuths:
        running = running + jnp.where(lane >= reach, pltpu.roll(running, reach, 1), 0.0)
        reach *= 2
    everything = jnp.sum(jnp.where(at_end, running, 0.0), axis=1, keepdims=True)
    totals[az] = jnp.broadcast_to(everything, (8, 128))

    def send_total(turn):
        peer = lax.rem(az + turn, n_az)
        return push(totals.at[az], totals.at[az], total_send.at[turn], total_recv.at[az], {"az": peer})

    def take_total(turn):
        peer = lax.rem(az + turn, n_az)
        return push(totals.at[peer], totals.at[peer], total_send.at[turn], total_recv.at[peer], {"az": peer})

    for turn in range(1, n_az):
        send_total(turn).start()
    for turn in range(1, n_az):
        take_total(turn).wait_recv()
    offset = jnp.zeros((8, 128), jnp.float32)
    for place in range(n_az):
        offset = offset + jnp.where(place < az, totals[place], 0.0)
    angle = offset[:, 0:1] + running - slope
    cosine, sine = jnp.cos(angle)[0:1], jnp.sin(angle)[0:1]

    def turn_rows(k, carry):
        at = pl.ds(k * 16, 16)
        re = out_re[at, :].astype(jnp.float32)
        im = out_im[at, :].astype(jnp.float32)
        out_re[at, :] = (re * cosine + im * sine).astype(jnp.bfloat16)
        out_im[at, :] = (im * cosine - re * sine).astype(jnp.bfloat16)
        return carry

    lax.fori_loop(0, cells // 16, turn_rows, 0)

    send_column.wait_send()
    for turn in range(1, n_rng):
        send_sums(turn).wait_send()
    for turn in range(1, n_az):
        send_total(turn).wait_send()

    def ended(slot, carry):
        where = slot // 2

        @pl.when(slot % 2 == core)
        def _():
            along(inner(slot), slot, SIBLING).wait_send()

            @pl.when((where <= chip) & (chip + 1 < chips))
            def _():
                along(inner(slot), slot, RIGHT).wait_send()

            @pl.when((where >= chip) & (chip > 0))
            def _():
                along(inner(slot), slot, LEFT).wait_send()

        @pl.when(rng + 1 < n_rng)
        def _():
            edge_low(inner(slot), slot).wait_send()

        @pl.when(rng > 0)
        def _():
            edge_high(inner(slot), slot).wait_send()

        return carry

    lax.fori_loop(0, n_az, ended, 0)


def per_device(echoes, owner_map, band_start, interp, steer_phase):
    n_rng, n_az = lax.axis_size("rng"), lax.axis_size("az")
    pings = owner_map.shape[0]
    blocks = band_start.shape[0]
    echo = echoes.reshape(echoes.shape[1] * echoes.shape[2], echoes.shape[3])
    interp = interp[:, 0]
    rows, width = echo.shape
    cells, band = interp.shape[1:]
    azimuths = steer_phase.shape[2]
    hits = owner_map[None, :] == jnp.arange(n_az, dtype=jnp.int32)[:, None]
    ping_of = jnp.sum(jnp.where(hits, jnp.arange(pings, dtype=jnp.int32)[None, :], 0), axis=1)
    used = jnp.any(hits, axis=1).astype(jnp.float32)
    nominal = jnp.arange(blocks, dtype=jnp.int32) * (width // blocks)
    shift = band_start[:, 0, :] - nominal[:, None]
    span = band + 2 * GUARD
    smem = pl.BlockSpec(memory_space=pltpu.SMEM)
    anywhere = pl.BlockSpec(memory_space=pl.ANY)
    vmem = pl.BlockSpec(memory_space=pltpu.VMEM)
    part = jax.ShapeDtypeStruct((cells, azimuths), jnp.bfloat16)
    dma = pltpu.SemaphoreType.DMA
    re, im = pl.pallas_call(
        functools.partial(kernel, n_rng, n_az, pings, blocks),
        out_shape=(part, part),
        in_specs=[smem, smem, smem, anywhere, anywhere, anywhere],
        out_specs=(vmem, vmem),
        scratch_shapes=[
            pltpu.VMEM((n_az, rows, width + 2 * GUARD), jnp.bfloat16),
            pltpu.VMEM(interp.shape, jnp.bfloat16),
            pltpu.VMEM(steer_phase.shape, jnp.float32),
            pltpu.VMEM((n_az, cells, span), jnp.bfloat16),
            pltpu.VMEM((n_az // 2, 2 * rows, 2 * azimuths), jnp.bfloat16),
            pltpu.VMEM((cells, 2 * rows), jnp.bfloat16),
            pltpu.VMEM((cells, 2 * azimuths), jnp.float32),
            pltpu.VMEM((2, 8, cells), jnp.float32),
            pltpu.VMEM((n_rng, 8, azimuths), jnp.float32),
            pltpu.VMEM((n_az, 8, 128), jnp.float32),
            dma((3,)), dma((5, n_az)), dma((3, n_az)), dma((2,)),
            dma((n_rng,)), dma((n_rng,)), dma((n_az,)), dma((n_az,)),
        ],
        compiler_params=pltpu.CompilerParams(
            collective_id=0, has_side_effects=True, vmem_limit_bytes=56 * 1024 * 1024
        ),
    )(ping_of, used, shift, echo, interp, steer_phase)
    return jnp.stack([re, im], axis=1)


def solution(mesh):
    in_specs = (
        P("az", None, None, "rng"),
        P(),
        P("rng", "az", None),
        P(None, "az", "rng", None),
        P(None, None, "az"),
    )
    out_specs = P("rng", None, "az")
    return jax.shard_map(
        per_device, mesh=mesh, in_specs=in_specs, out_specs=out_specs, check_vma=False
    )
```

```python
import functools

import jax
import jax.numpy as jnp
from jax import lax
from jax.experimental import pallas as pl
from jax.experimental.pallas import tpu as pltpu
from jax.sharding import PartitionSpec as P

GUARD = 128
MESH = pl.DeviceIdType.MESH
RIGHT, LEFT, SIBLING, LOW, HIGH = range(5)


def sine_cosine(x):
    turns = jnp.floor(x * 0.6366197723675814 + 0.5)
    r = x - turns * 1.5703125
    r = r - turns * 4.837512969970703e-4
    r = r - turns * 7.549789948768648e-8
    quadrant = turns.astype(jnp.int32)
    r2 = r * r
    s = r + r * r2 * (-1 / 6 + r2 * (1 / 120 + r2 * (-1 / 5040 + r2 * (1 / 362880))))
    c = 1.0 + r2 * (-0.5 + r2 * (1 / 24 + r2 * (-1 / 720 + r2 * (1 / 40320))))
    odd = (quadrant & 1) == 1
    sine = jnp.where(odd, c, s)
    cosine = jnp.where(odd, s, c)
    sine = jnp.where((quadrant & 2) == 2, -sine, sine)
    cosine = jnp.where(((quadrant + 1) & 2) == 2, -cosine, cosine)
    return sine, cosine


def transposed_dot(a, b):
    return lax.dot_general(a, b, (((1,), (1,)), ((), ())), preferred_element_type=jnp.float32)


def kernel(
    n_rng, n_az, pings, blocks,
    owner, start, echo, interp, phase,
    out_re, out_im, turn_of,
    window, interp_v, phase_v, shifted, steer, focus, image, column, sums, totals,
    load_sem, send_sem, recv_sem, column_sem, sum_send, sum_recv, total_send, total_recv,
):
    rng, az = lax.axis_index("rng"), lax.axis_index("az")
    chips = n_az // 2
    chip, core = az // 2, az % 2
    width = echo.shape[1]
    rows = echo.shape[0]
    half = rows // 2
    cells = interp.shape[1]
    band = interp.shape[2]
    azimuths = phase.shape[2]
    block = cells // blocks
    step = width // blocks
    scale = 1.0 / (pings * half) ** 0.5

    barrier = pltpu.get_barrier_semaphore()
    for turn in range(1, n_rng):
        pl.semaphore_signal(barrier, inc=1, device_id={"rng": lax.rem(rng + turn, n_rng)}, device_id_type=MESH)
    for turn in range(1, n_az):
        pl.semaphore_signal(barrier, inc=1, device_id={"az": lax.rem(az + turn, n_az)}, device_id_type=MESH)
    pl.semaphore_wait(barrier, n_rng + n_az - 2)

    def inner(slot):
        return window.at[slot, :, pl.ds(GUARD, width)]

    def push(src, dst, sent, got, target):
        return pltpu.make_async_remote_copy(
            src_ref=src, dst_ref=dst, send_sem=sent, recv_sem=got, device_id=target, device_id_type=MESH
        )

    def along(src, slot, kind):
        target = {RIGHT: az + 2, LEFT: az - 2, SIBLING: az + 1 - 2 * core}[kind]
        return push(src, inner(slot), send_sem.at[kind, slot], recv_sem.at[0, slot], {"az": target})

    def edge_low(src, slot):
        return push(
            src.at[:, pl.ds(width - GUARD, GUARD)], window.at[slot, :, pl.ds(0, GUARD)],
            send_sem.at[LOW, slot], recv_sem.at[1, slot], {"rng": rng + 1},
        )

    def edge_high(src, slot):
        return push(
            src.at[:, pl.ds(0, GUARD)], window.at[slot, :, pl.ds(GUARD + width, GUARD)],
            send_sem.at[HIGH, slot], recv_sem.at[2, slot], {"rng": rng - 1},
        )

    def send_edges(src, slot):
        @pl.when(rng + 1 < n_rng)
        def _():
            edge_low(src, slot).start()

        @pl.when(rng > 0)
        def _():
            edge_high(src, slot).start()

    def wait_edges(slot):
        @pl.when(rng > 0)
        def _():
            edge_low(inner(slot), slot).wait_recv()

        @pl.when(rng + 1 < n_rng)
        def _():
            edge_high(inner(slot), slot).wait_recv()

    @pl.when(chip + 1 < chips)
    def _():
        along(echo, az, RIGHT).start()

    @pl.when(chip > 0)
    def _():
        along(echo, az, LEFT).start()

    along(echo, az, SIBLING).start()
    send_edges(echo, az)
    own_copy = pltpu.make_async_copy(echo, inner(az), load_sem.at[0])
    own_copy.start()
    interp_copy = pltpu.make_async_copy(interp, interp_v, load_sem.at[1])
    interp_copy.start()
    phase_copy = pltpu.make_async_copy(phase, phase_v, load_sem.at[2])
    phase_copy.start()

    @pl.when(rng == 0)
    def _():
        window[:, :, 0:GUARD] = jnp.zeros((n_az, rows, GUARD), window.dtype)

    @pl.when(rng == n_rng - 1)
    def _():
        window[:, :, GUARD + width:] = jnp.zeros((n_az, rows, GUARD), window.dtype)

    def prepare(where):
        for side in range(2):
            slot = 2 * where + side
            ping = jnp.int32(0)
            used = jnp.float32(0.0)
            for p in range(pings):
                hit = owner[p] == slot
                ping = jnp.where(hit, p, ping)
                used = jnp.where(hit, 1.0, used)

            def one_block(g, carry):
                part = interp_v[ping, pl.ds(g * block, block), :].astype(jnp.float32)
                if n_az != pings:
                    part = part * used
                move = start[g, 0, ping] - g * step
                lane = lax.broadcasted_iota(jnp.int32, (block, band), 1)
                part = pltpu.roll(part, lax.rem(move, band), 1)
                near = lane >= move
                shifted[slot, g, block:, :] = jnp.where(near, part, 0.0).astype(jnp.bfloat16)
                shifted[slot, g + 1, 0:block, :] = jnp.where(near, 0.0, part).astype(jnp.bfloat16)
                return carry

            lax.fori_loop(0, blocks, one_block, 0, unroll=2)

            def one_rows(k, carry):
                sine, cosine = sine_cosine(phase_v[ping, pl.ds(k * 16, 16), :])
                sine, cosine = sine * scale, cosine * scale
                top = pl.ds(side * rows + k * 16, 16)
                low = pl.ds(side * rows + half + k * 16, 16)
                steer[where, top, 0:azimuths] = cosine.astype(jnp.bfloat16)
                steer[where, top, azimuths:] = sine.astype(jnp.bfloat16)
                steer[where, low, 0:azimuths] = (-sine).astype(jnp.bfloat16)
                steer[where, low, azimuths:] = cosine.astype(jnp.bfloat16)
                return carry

            lax.fori_loop(0, half // 16, one_rows, 0)

    def compute(where, first):
        for side in range(2):
            slot = 2 * where + side
            columns = slice(side * rows, (side + 1) * rows)
            before = None
            for k in range(blocks + 1):
                low = block if k == 0 else 0
                high = block if k == blocks else 2 * block
                got = transposed_dot(shifted[slot, k, low:high, :], window[slot, :, k * step:(k + 1) * step])
                if k > 0:
                    focus[(k - 1) * block:k * block, columns] = (before + got[0:block]).astype(jnp.bfloat16)
                before = got[block - low:]

        def one_part(k, carry):
            columns = pl.ds(k * 256, 256)
            got = jnp.dot(focus[...], steer[where, :, columns], preferred_element_type=jnp.float32)
            if first:
                image[:, columns] = got
            else:
                image[:, columns] = image[:, columns] + got
            return carry

        lax.fori_loop(0, 2 * azimuths // 256, one_part, 0)

    def sides_at(distance):
        left, right = chip - distance, chip + distance
        return ((left, left >= 0, RIGHT), (right, right < chips, LEFT))

    def prepare_at(distance):
        for where, there, _ in sides_at(distance):
            @pl.when(there)
            def _():
                prepare(where)

    interp_copy.wait()
    phase_copy.wait()
    prepare(chip)
    own_copy.wait()
    sibling = 2 * chip + 1 - core
    along(inner(sibling), sibling, SIBLING).wait_recv()
    send_edges(inner(sibling), sibling)
    prepare_at(1)

    def at_distance(distance, carry):
        sides = sides_at(distance)
        for where, there, onward in sides:
            @pl.when(there)
            def _():
                slot = 2 * where + core
                along(inner(slot), slot, onward).wait_recv()
                more = chip + 1 < chips if onward == RIGHT else chip > 0

                @pl.when(more)
                def _():
                    along(inner(slot), slot, onward).start()

                along(inner(slot), slot, SIBLING).start()
                send_edges(inner(slot), slot)

        @pl.when(distance == 1)
        def _():
            wait_edges(az)
            wait_edges(sibling)
            compute(chip, True)

        for where, there, _ in sides:
            @pl.when(there)
            def _():
                slot = 2 * where + 1 - core
                along(inner(slot), slot, SIBLING).wait_recv()
                send_edges(inner(slot), slot)

        for where, there, _ in sides:
            @pl.when(there)
            def _():
                wait_edges(2 * where)
                wait_edges(2 * where + 1)
                compute(where, False)

        prepare_at(distance + 1)
        return carry

    lax.fori_loop(1, chips, at_distance, 0)

    def one_group(k, carry):
        cross_re, cross_im, power = carry
        at = pl.ds(k * 16, 16)
        re16 = image[at, 0:azimuths].astype(jnp.bfloat16)
        im16 = image[at, azimuths:].astype(jnp.bfloat16)
        out_re[at, :] = re16
        out_im[at, :] = im16
        re, im = re16.astype(jnp.float32), im16.astype(jnp.float32)
        re_next = pltpu.roll(re, azimuths - 1, 1)
        im_next = pltpu.roll(im, azimuths - 1, 1)

        def fold(x):
            return x[0:8] + x[8:16]

        return (
            cross_re + fold(re * re_next + im * im_next),
            cross_im + fold(re * im_next - im * re_next),
            power + fold(re * re + im * im),
        )

    zero = jnp.zeros((8, azimuths), jnp.float32)
    cross_re, cross_im, power = lax.fori_loop(0, cells // 16, one_group, (zero, zero, zero), unroll=2)

    row16 = lax.broadcasted_iota(jnp.int32, (16, 128), 0)
    lane16 = lax.broadcasted_iota(jnp.int32, (16, 128), 1)

    def pick(row, lane):
        return jnp.where((row16 == row) & (lane16 == lane), 1.0, 0.0).astype(jnp.bfloat16)

    head = transposed_dot(pick(0, 0), out_re[:, 0:128]) + transposed_dot(pick(1, 0), out_im[:, 0:128])
    column[0] = head[0:8]
    send_column = push(
        column.at[0], column.at[1], column_sem.at[0], column_sem.at[1], {"az": lax.rem(az + n_az - 1, n_az)}
    )
    send_column.start()
    tail_re = transposed_dot(pick(0, 127), out_re[:, azimuths - 128:])
    tail_im = transposed_dot(pick(0, 127), out_im[:, azimuths - 128:])
    send_column.wait_recv()
    next_re, next_im = column[1, 0:1, :], column[1, 1:2, :]
    last_re, last_im = tail_re[0:1], tail_im[0:1]
    inside = jnp.where(az == n_az - 1, 0.0, 1.0)
    edge_re = jnp.sum(last_re * next_re + last_im * next_im, axis=1, keepdims=True) * inside
    edge_im = jnp.sum(last_re * next_im - last_im * next_re, axis=1, keepdims=True) * inside

    lane = lax.broadcasted_iota(jnp.int32, (8, azimuths), 1)
    row = lax.broadcasted_iota(jnp.int32, (8, azimuths), 0)
    at_end = lane == azimuths - 1
    cross_re = jnp.where(at_end, edge_re, jnp.sum(cross_re, axis=0, keepdims=True))
    cross_im = jnp.where(at_end, edge_im, jnp.sum(cross_im, axis=0, keepdims=True))
    power = jnp.sum(power, axis=0, keepdims=True)
    sums[rng] = jnp.where(row == 0, cross_re, jnp.where(row == 1, cross_im, power))

    def send_sums(turn):
        peer = lax.rem(rng + turn, n_rng)
        return push(sums.at[rng], sums.at[rng], sum_send.at[turn], sum_recv.at[rng], {"rng": peer})

    def take_sums(turn):
        peer = lax.rem(rng + turn, n_rng)
        return push(sums.at[peer], sums.at[peer], sum_send.at[turn], sum_recv.at[peer], {"rng": peer})

    for turn in range(1, n_rng):
        send_sums(turn).start()
    for turn in range(1, n_rng):
        take_sums(turn).wait_recv()
    total = sums[0]
    for turn in range(1, n_rng):
        total = total + sums[turn]
    cross_re, cross_im, power = total[0:1], total[1:2], total[2:3] + 1e-06
    slope = cross_im / power
    slope = slope + (cross_im * jnp.cos(slope) - cross_re * jnp.sin(slope)) / power
    slope = jnp.broadcast_to(slope, (8, azimuths))
    running = slope
    reach = 1
    while reach < azimuths:
        running = running + jnp.where(lane >= reach, pltpu.roll(running, reach, 1), 0.0)
        reach *= 2
    everything = jnp.sum(jnp.where(at_end, running, 0.0), axis=1, keepdims=True)
    totals[az] = jnp.broadcast_to(everything, (8, 128))

    def send_total(turn):
        peer = lax.rem(az + turn, n_az)
        return push(totals.at[az], totals.at[az], total_send.at[turn], total_recv.at[az], {"az": peer})

    def take_total(turn):
        peer = lax.rem(az + turn, n_az)
        return push(totals.at[peer], totals.at[peer], total_send.at[turn], total_recv.at[peer], {"az": peer})

    for turn in range(1, n_az):
        send_total(turn).start()
    for turn in range(1, n_az):
        take_total(turn).wait_recv()
    offset = jnp.zeros((8, 128), jnp.float32)
    for place in range(n_az):
        offset = offset + jnp.where(place < az, totals[place], 0.0)
    angle = offset[:, 0:1] + running - slope
    turn_of[0] = jnp.cos(angle)
    turn_of[1] = jnp.sin(angle)

    send_column.wait_send()
    for turn in range(1, n_rng):
        send_sums(turn).wait_send()
    for turn in range(1, n_az):
        send_total(turn).wait_send()

    def ended(slot, carry):
        where = slot // 2

        @pl.when(slot % 2 == core)
        def _():
            along(inner(slot), slot, SIBLING).wait_send()

            @pl.when((where <= chip) & (chip + 1 < chips))
            def _():
                along(inner(slot), slot, RIGHT).wait_send()

            @pl.when((where >= chip) & (chip > 0))
            def _():
                along(inner(slot), slot, LEFT).wait_send()

        @pl.when(rng + 1 < n_rng)
        def _():
            edge_low(inner(slot), slot).wait_send()

        @pl.when(rng > 0)
        def _():
            edge_high(inner(slot), slot).wait_send()

        return carry

    lax.fori_loop(0, n_az, ended, 0)


def turned(turn_of, in_re, in_im, out):
    cosine, sine = turn_of[0, 0:1, :], turn_of[1, 0:1, :]
    re, im = in_re[...].astype(jnp.float32), in_im[...].astype(jnp.float32)
    out[...] = jnp.stack([re * cosine + im * sine, im * cosine - re * sine], axis=1).astype(jnp.bfloat16)


def per_device(echoes, owner_map, band_start, interp, steer_phase):
    n_rng, n_az = lax.axis_size("rng"), lax.axis_size("az")
    pings = owner_map.shape[0]
    blocks = band_start.shape[0]
    echo = echoes.reshape(echoes.shape[1] * echoes.shape[2], echoes.shape[3])
    interp = interp[:, 0]
    rows, width = echo.shape
    cells, band = interp.shape[1:]
    azimuths = steer_phase.shape[2]
    smem = pl.BlockSpec(memory_space=pltpu.SMEM)
    anywhere = pl.BlockSpec(memory_space=pl.ANY)
    vmem = pl.BlockSpec(memory_space=pltpu.VMEM)
    part = jax.ShapeDtypeStruct((cells, azimuths), jnp.bfloat16)
    dma = pltpu.SemaphoreType.DMA
    re, im, turn_of = pl.pallas_call(
        functools.partial(kernel, n_rng, n_az, pings, blocks),
        out_shape=(part, part, jax.ShapeDtypeStruct((2, 8, azimuths), jnp.float32)),
        in_specs=[smem, smem, anywhere, anywhere, anywhere],
        out_specs=(vmem, vmem, vmem),
        scratch_shapes=[
            pltpu.VMEM((n_az, rows, width + 2 * GUARD), jnp.bfloat16),
            pltpu.VMEM(interp.shape, jnp.bfloat16),
            pltpu.VMEM(steer_phase.shape, jnp.float32),
            pltpu.VMEM((n_az, blocks + 1, 2 * cells // blocks, band), jnp.bfloat16),
            pltpu.VMEM((n_az // 2, 2 * rows, 2 * azimuths), jnp.bfloat16),
            pltpu.VMEM((cells, 2 * rows), jnp.bfloat16),
            pltpu.VMEM((cells, 2 * azimuths), jnp.float32),
            pltpu.VMEM((2, 8, cells), jnp.float32),
            pltpu.VMEM((n_rng, 8, azimuths), jnp.float32),
            pltpu.VMEM((n_az, 8, 128), jnp.float32),
            dma((3,)), dma((5, n_az)), dma((3, n_az)), dma((2,)),
            dma((n_rng,)), dma((n_rng,)), dma((n_az,)), dma((n_az,)),
        ],
        compiler_params=pltpu.CompilerParams(
            collective_id=0, has_side_effects=True, vmem_limit_bytes=56 * 1024 * 1024
        ),
    )(owner_map, band_start, echo, interp, steer_phase)
    lines = cells // 6
    piece = pl.BlockSpec((lines, azimuths), lambda i: (i, 0))
    return pl.pallas_call(
        turned,
        grid=(cells // lines,),
        out_shape=jax.ShapeDtypeStruct((cells, 2, azimuths), jnp.bfloat16),
        in_specs=[pl.BlockSpec((2, 8, azimuths), lambda i: (0, 0, 0)), piece, piece],
        out_specs=pl.BlockSpec((lines, 2, azimuths), lambda i: (i, 0, 0)),
    )(turn_of, re, im)


def solution(mesh):
    in_specs = (
        P("az", None, None, "rng"),
        P(),
        P("rng", "az", None),
        P(None, "az", "rng", None),
        P(None, None, "az"),
    )
    out_specs = P("rng", None, "az")
    return jax.shard_map(
        per_device, mesh=mesh, in_specs=in_specs, out_specs=out_specs, check_vma=False
    )
```

```python
import functools

import jax
import jax.numpy as jnp
from jax import lax
from jax.experimental import pallas as pl
from jax.experimental.pallas import tpu as pltpu
from jax.sharding import PartitionSpec as P

GUARD = 128
MESH = pl.DeviceIdType.MESH
RIGHT, LEFT, SIBLING, LOW, HIGH = 0, 2, 4, 6, 7
HALVES = 2


def sine_cosine(x):
    turns = jnp.floor(x * 0.6366197723675814 + 0.5)
    r = x - turns * 1.5703125
    r = r - turns * 4.837512969970703e-4
    r = r - turns * 7.549789948768648e-8
    quadrant = turns.astype(jnp.int32)
    r2 = r * r
    s = r + r * r2 * (-1 / 6 + r2 * (1 / 120 + r2 * (-1 / 5040 + r2 * (1 / 362880))))
    c = 1.0 + r2 * (-0.5 + r2 * (1 / 24 + r2 * (-1 / 720 + r2 * (1 / 40320))))
    odd = (quadrant & 1) == 1
    sine = jnp.where(odd, c, s)
    cosine = jnp.where(odd, s, c)
    sine = jnp.where((quadrant & 2) == 2, -sine, sine)
    cosine = jnp.where(((quadrant + 1) & 2) == 2, -cosine, cosine)
    return sine, cosine


def transposed_dot(a, b):
    return lax.dot_general(a, b, (((1,), (1,)), ((), ())), preferred_element_type=jnp.float32)


def kernel(
    n_rng, n_az, pings, blocks,
    owner, start, echo, interp, phase,
    out_re, out_im, turn_of,
    window, interp_v, phase_v, shifted, steer, focus, image, column, sums, totals,
    load_sem, send_sem, recv_sem, column_sem, sum_send, sum_recv, total_send, total_recv,
):
    rng, az = lax.axis_index("rng"), lax.axis_index("az")
    chips = n_az // 2
    chip, core = az // 2, az % 2
    width = echo.shape[1]
    rows = echo.shape[0]
    half = rows // 2
    cells = interp.shape[1]
    band = interp.shape[2]
    azimuths = phase.shape[2]
    block = cells // blocks
    step = width // blocks
    scale = 1.0 / (pings * half) ** 0.5

    barrier = pltpu.get_barrier_semaphore()
    for turn in range(1, n_rng):
        pl.semaphore_signal(barrier, inc=1, device_id={"rng": lax.rem(rng + turn, n_rng)}, device_id_type=MESH)
    for turn in range(1, n_az):
        pl.semaphore_signal(barrier, inc=1, device_id={"az": lax.rem(az + turn, n_az)}, device_id_type=MESH)
    pl.semaphore_wait(barrier, n_rng + n_az - 2)

    def inner(slot):
        return window.at[slot, :, pl.ds(GUARD, width)]

    def push(src, dst, sent, got, target):
        return pltpu.make_async_remote_copy(
            src_ref=src, dst_ref=dst, send_sem=sent, recv_sem=got, device_id=target, device_id_type=MESH
        )

    def along(src, slot, kind, part):
        target = {RIGHT: az + 2, LEFT: az - 2, SIBLING: az + 1 - 2 * core}[kind]
        lines = pl.ds(part * half, half)
        return push(
            src.at[lines, :], inner(slot).at[lines, :],
            send_sem.at[kind + part, slot], recv_sem.at[part, slot], {"az": target},
        )

    def edge_low(src, slot):
        return push(
            src.at[:, pl.ds(width - GUARD, GUARD)], window.at[slot, :, pl.ds(0, GUARD)],
            send_sem.at[LOW, slot], recv_sem.at[HALVES, slot], {"rng": rng + 1},
        )

    def edge_high(src, slot):
        return push(
            src.at[:, pl.ds(0, GUARD)], window.at[slot, :, pl.ds(GUARD + width, GUARD)],
            send_sem.at[HIGH, slot], recv_sem.at[HALVES + 1, slot], {"rng": rng - 1},
        )

    def send_edges(src, slot):
        @pl.when(rng + 1 < n_rng)
        def _():
            edge_low(src, slot).start()

        @pl.when(rng > 0)
        def _():
            edge_high(src, slot).start()

    def wait_edges(slot):
        @pl.when(rng > 0)
        def _():
            edge_low(inner(slot), slot).wait_recv()

        @pl.when(rng + 1 < n_rng)
        def _():
            edge_high(inner(slot), slot).wait_recv()

    for part in range(HALVES):
        @pl.when(chip + 1 < chips)
        def _():
            along(echo, az, RIGHT, part).start()

        @pl.when(chip > 0)
        def _():
            along(echo, az, LEFT, part).start()

        along(echo, az, SIBLING, part).start()

    send_edges(echo, az)
    own_copy = pltpu.make_async_copy(echo, inner(az), load_sem.at[0])
    own_copy.start()
    interp_copy = pltpu.make_async_copy(interp, interp_v, load_sem.at[1])
    interp_copy.start()
    phase_copy = pltpu.make_async_copy(phase, phase_v, load_sem.at[2])
    phase_copy.start()

    @pl.when(rng == 0)
    def _():
        window[:, :, 0:GUARD] = jnp.zeros((n_az, rows, GUARD), window.dtype)

    @pl.when(rng == n_rng - 1)
    def _():
        window[:, :, GUARD + width:] = jnp.zeros((n_az, rows, GUARD), window.dtype)

    def prepare(where):
        for side in range(2):
            slot = 2 * where + side
            ping = jnp.int32(0)
            used = jnp.float32(0.0)
            for p in range(pings):
                hit = owner[p] == slot
                ping = jnp.where(hit, p, ping)
                used = jnp.where(hit, 1.0, used)

            def one_block(g, carry):
                part = interp_v[ping, pl.ds(g * block, block), :].astype(jnp.float32)
                if n_az != pings:
                    part = part * used
                move = start[g, 0, ping] - g * step
                lane = lax.broadcasted_iota(jnp.int32, (block, band), 1)
                part = pltpu.roll(part, lax.rem(move, band), 1)
                near = lane >= move
                shifted[slot, g, block:, :] = jnp.where(near, part, 0.0).astype(jnp.bfloat16)
                shifted[slot, g + 1, 0:block, :] = jnp.where(near, 0.0, part).astype(jnp.bfloat16)
                return carry

            lax.fori_loop(0, blocks, one_block, 0, unroll=2)

            def one_rows(k, carry):
                sine, cosine = sine_cosine(phase_v[ping, pl.ds(k * 16, 16), :])
                sine, cosine = sine * scale, cosine * scale
                top = pl.ds(side * rows + k * 16, 16)
                low = pl.ds(side * rows + half + k * 16, 16)
                steer[where, top, 0:azimuths] = cosine.astype(jnp.bfloat16)
                steer[where, top, azimuths:] = sine.astype(jnp.bfloat16)
                steer[where, low, 0:azimuths] = (-sine).astype(jnp.bfloat16)
                steer[where, low, azimuths:] = cosine.astype(jnp.bfloat16)
                return carry

            lax.fori_loop(0, half // 16, one_rows, 0)

    def compute(where, first):
        for side in range(2):
            slot = 2 * where + side
            columns = slice(side * rows, (side + 1) * rows)
            before = None
            for k in range(blocks + 1):
                low = block if k == 0 else 0
                high = block if k == blocks else 2 * block
                got = transposed_dot(shifted[slot, k, low:high, :], window[slot, :, k * step:(k + 1) * step])
                if k > 0:
                    focus[(k - 1) * block:k * block, columns] = (before + got[0:block]).astype(jnp.bfloat16)
                before = got[block - low:]

        def one_part(k, carry):
            columns = pl.ds(k * 256, 256)
            got = jnp.dot(focus[...], steer[where, :, columns], preferred_element_type=jnp.float32)
            if first:
                image[:, columns] = got
            else:
                image[:, columns] = image[:, columns] + got
            return carry

        lax.fori_loop(0, 2 * azimuths // 256, one_part, 0)

    def sides_at(distance):
        left, right = chip - distance, chip + distance
        return ((left, left >= 0, RIGHT), (right, right < chips, LEFT))

    def prepare_at(distance):
        for where, there, _ in sides_at(distance):
            @pl.when(there)
            def _():
                prepare(where)

    def sides_at(distance):
        left, right = chip - distance, chip + distance
        return ((left, left >= 0, RIGHT), (right, right < chips, LEFT))

    def forward(distance, part):
        for where, there, onward in sides_at(distance):
            @pl.when(there)
            def _():
                slot = 2 * where + core
                along(inner(slot), slot, onward, part).wait_recv()
                more = chip + 1 < chips if onward == RIGHT else chip > 0

                @pl.when(more)
                def _():
                    along(inner(slot), slot, onward, part).start()

                along(inner(slot), slot, SIBLING, part).start()
                if part == HALVES - 1:
                    send_edges(inner(slot), slot)

    def from_sibling(where):
        slot = 2 * where + 1 - core
        for part in range(HALVES):
            along(inner(slot), slot, SIBLING, part).wait_recv()
        send_edges(inner(slot), slot)

    def finish(where, first):
        wait_edges(2 * where)
        wait_edges(2 * where + 1)
        compute(where, first)

    interp_copy.wait()
    phase_copy.wait()
    prepare(chip)
    own_copy.wait()
    from_sibling(chip)
    finish(chip, True)
    between = (chip > 0) & (chip + 1 < chips)

    def at_distance(distance, carry):
        forward(distance, 0)
        early = (distance == 1) | jnp.logical_not(between)
        sides = sides_at(distance)
        for where, there, _ in sides:
            @pl.when(there & early)
            def _():
                prepare(where)

        forward(distance, 1)
        for where, there, _ in sides:
            @pl.when(there & jnp.logical_not(early))
            def _():
                prepare(where)

        for where, there, _ in sides:
            @pl.when(there)
            def _():
                from_sibling(where)

        for where, there, _ in sides:
            @pl.when(there)
            def _():
                finish(where, False)

        return carry

    lax.fori_loop(1, chips, at_distance, 0)

    def one_group(k, carry):
        cross_re, cross_im, power = carry
        at = pl.ds(k * 16, 16)
        re16 = image[at, 0:azimuths].astype(jnp.bfloat16)
        im16 = image[at, azimuths:].astype(jnp.bfloat16)
        out_re[at, :] = re16
        out_im[at, :] = im16
        re, im = re16.astype(jnp.float32), im16.astype(jnp.float32)
        re_next = pltpu.roll(re, azimuths - 1, 1)
        im_next = pltpu.roll(im, azimuths - 1, 1)

        def fold(x):
            return x[0:8] + x[8:16]

        return (
            cross_re + fold(re * re_next + im * im_next),
            cross_im + fold(re * im_next - im * re_next),
            power + fold(re * re + im * im),
        )

    zero = jnp.zeros((8, azimuths), jnp.float32)
    cross_re, cross_im, power = lax.fori_loop(0, cells // 16, one_group, (zero, zero, zero), unroll=2)

    row16 = lax.broadcasted_iota(jnp.int32, (16, 128), 0)
    lane16 = lax.broadcasted_iota(jnp.int32, (16, 128), 1)

    def pick(row, lane):
        return jnp.where((row16 == row) & (lane16 == lane), 1.0, 0.0).astype(jnp.bfloat16)

    head = transposed_dot(pick(0, 0), out_re[:, 0:128]) + transposed_dot(pick(1, 0), out_im[:, 0:128])
    column[0] = head[0:8]
    send_column = push(
        column.at[0], column.at[1], column_sem.at[0], column_sem.at[1], {"az": lax.rem(az + n_az - 1, n_az)}
    )
    send_column.start()
    tail_re = transposed_dot(pick(0, 127), out_re[:, azimuths - 128:])
    tail_im = transposed_dot(pick(0, 127), out_im[:, azimuths - 128:])
    send_column.wait_recv()
    next_re, next_im = column[1, 0:1, :], column[1, 1:2, :]
    last_re, last_im = tail_re[0:1], tail_im[0:1]
    inside = jnp.where(az == n_az - 1, 0.0, 1.0)
    edge_re = jnp.sum(last_re * next_re + last_im * next_im, axis=1, keepdims=True) * inside
    edge_im = jnp.sum(last_re * next_im - last_im * next_re, axis=1, keepdims=True) * inside

    lane = lax.broadcasted_iota(jnp.int32, (8, azimuths), 1)
    row = lax.broadcasted_iota(jnp.int32, (8, azimuths), 0)
    at_end = lane == azimuths - 1
    cross_re = jnp.where(at_end, edge_re, jnp.sum(cross_re, axis=0, keepdims=True))
    cross_im = jnp.where(at_end, edge_im, jnp.sum(cross_im, axis=0, keepdims=True))
    power = jnp.sum(power, axis=0, keepdims=True)
    sums[rng] = jnp.where(row == 0, cross_re, jnp.where(row == 1, cross_im, power))

    def send_sums(turn):
        peer = lax.rem(rng + turn, n_rng)
        return push(sums.at[rng], sums.at[rng], sum_send.at[turn], sum_recv.at[rng], {"rng": peer})

    def take_sums(turn):
        peer = lax.rem(rng + turn, n_rng)
        return push(sums.at[peer], sums.at[peer], sum_send.at[turn], sum_recv.at[peer], {"rng": peer})

    for turn in range(1, n_rng):
        send_sums(turn).start()
    for turn in range(1, n_rng):
        take_sums(turn).wait_recv()
    total = sums[0]
    for turn in range(1, n_rng):
        total = total + sums[turn]
    cross_re, cross_im, power = total[0:1], total[1:2], total[2:3] + 1e-06
    slope = cross_im / power
    slope = slope + (cross_im * jnp.cos(slope) - cross_re * jnp.sin(slope)) / power
    slope = jnp.broadcast_to(slope, (8, azimuths))
    running = slope
    reach = 1
    while reach < azimuths:
        running = running + jnp.where(lane >= reach, pltpu.roll(running, reach, 1), 0.0)
        reach *= 2
    everything = jnp.sum(jnp.where(at_end, running, 0.0), axis=1, keepdims=True)
    totals[az] = jnp.broadcast_to(everything, (8, 128))

    def send_total(turn):
        peer = lax.rem(az + turn, n_az)
        return push(totals.at[az], totals.at[az], total_send.at[turn], total_recv.at[az], {"az": peer})

    def take_total(turn):
        peer = lax.rem(az + turn, n_az)
        return push(totals.at[peer], totals.at[peer], total_send.at[turn], total_recv.at[peer], {"az": peer})

    for turn in range(1, n_az):
        send_total(turn).start()
    for turn in range(1, n_az):
        take_total(turn).wait_recv()
    offset = jnp.zeros((8, 128), jnp.float32)
    for place in range(n_az):
        offset = offset + jnp.where(place < az, totals[place], 0.0)
    angle = offset[:, 0:1] + running - slope
    turn_of[0] = jnp.cos(angle)
    turn_of[1] = jnp.sin(angle)

    send_column.wait_send()
    for turn in range(1, n_rng):
        send_sums(turn).wait_send()
    for turn in range(1, n_az):
        send_total(turn).wait_send()

    def ended(slot, carry):
        where = slot // 2
        for part in range(HALVES):
            @pl.when(slot % 2 == core)
            def _():
                along(inner(slot), slot, SIBLING, part).wait_send()

                @pl.when((where <= chip) & (chip + 1 < chips))
                def _():
                    along(inner(slot), slot, RIGHT, part).wait_send()

                @pl.when((where >= chip) & (chip > 0))
                def _():
                    along(inner(slot), slot, LEFT, part).wait_send()

        @pl.when(rng + 1 < n_rng)
        def _():
            edge_low(inner(slot), slot).wait_send()

        @pl.when(rng > 0)
        def _():
            edge_high(inner(slot), slot).wait_send()

        return carry

    lax.fori_loop(0, n_az, ended, 0)


def turned(turn_of, in_re, in_im, out, new_re, new_im):
    lines, azimuths = in_re.shape
    cosine, sine = turn_of[0, 0:1, :], turn_of[1, 0:1, :]

    def rotate(k, carry):
        at = pl.ds(k * 16, 16)
        re, im = in_re[at, :].astype(jnp.float32), in_im[at, :].astype(jnp.float32)
        new_re[at, :] = re * cosine + im * sine
        new_im[at, :] = im * cosine - re * sine
        return carry

    lax.fori_loop(0, lines // 16, rotate, 0, unroll=2)
    real = lax.broadcasted_iota(jnp.int32, (2, azimuths), 0) == 0

    def place(k, carry):
        pair = jnp.where(real, new_re[pl.ds(k, 1), :], new_im[pl.ds(k, 1), :])
        out[k] = pair.astype(jnp.bfloat16)
        return carry

    lax.fori_loop(0, lines, place, 0, unroll=16)


def per_device(echoes, owner_map, band_start, interp, steer_phase):
    n_rng, n_az = lax.axis_size("rng"), lax.axis_size("az")
    pings = owner_map.shape[0]
    blocks = band_start.shape[0]
    echo = echoes.reshape(echoes.shape[1] * echoes.shape[2], echoes.shape[3])
    interp = interp[:, 0]
    rows, width = echo.shape
    cells, band = interp.shape[1:]
    azimuths = steer_phase.shape[2]
    smem = pl.BlockSpec(memory_space=pltpu.SMEM)
    anywhere = pl.BlockSpec(memory_space=pl.ANY)
    vmem = pl.BlockSpec(memory_space=pltpu.VMEM)
    part = jax.ShapeDtypeStruct((cells, azimuths), jnp.bfloat16)
    dma = pltpu.SemaphoreType.DMA
    re, im, turn_of = pl.pallas_call(
        functools.partial(kernel, n_rng, n_az, pings, blocks),
        out_shape=(part, part, jax.ShapeDtypeStruct((2, 8, azimuths), jnp.float32)),
        in_specs=[smem, smem, anywhere, anywhere, anywhere],
        out_specs=(vmem, vmem, vmem),
        scratch_shapes=[
            pltpu.VMEM((n_az, rows, width + 2 * GUARD), jnp.bfloat16),
            pltpu.VMEM(interp.shape, jnp.bfloat16),
            pltpu.VMEM(steer_phase.shape, jnp.float32),
            pltpu.VMEM((n_az, blocks + 1, 2 * cells // blocks, band), jnp.bfloat16),
            pltpu.VMEM((n_az // 2, 2 * rows, 2 * azimuths), jnp.bfloat16),
            pltpu.VMEM((cells, 2 * rows), jnp.bfloat16),
            pltpu.VMEM((cells, 2 * azimuths), jnp.float32),
            pltpu.VMEM((2, 8, cells), jnp.float32),
            pltpu.VMEM((n_rng, 8, azimuths), jnp.float32),
            pltpu.VMEM((n_az, 8, 128), jnp.float32),
            dma((3,)), dma((3 * HALVES + 2, n_az)), dma((HALVES + 2, n_az)), dma((2,)),
            dma((n_rng,)), dma((n_rng,)), dma((n_az,)), dma((n_az,)),
        ],
        compiler_params=pltpu.CompilerParams(
            collective_id=0, has_side_effects=True, vmem_limit_bytes=56 * 1024 * 1024
        ),
    )(owner_map, band_start, echo, interp, steer_phase)
    lines = cells // 6
    piece = pl.BlockSpec((lines, azimuths), lambda i: (i, 0))
    return pl.pallas_call(
        turned,
        grid=(cells // lines,),
        out_shape=jax.ShapeDtypeStruct((cells, 2, azimuths), jnp.bfloat16),
        in_specs=[pl.BlockSpec((2, 8, azimuths), lambda i: (0, 0, 0)), piece, piece],
        out_specs=pl.BlockSpec((lines, 2, azimuths), lambda i: (i, 0, 0)),
        scratch_shapes=[pltpu.VMEM((lines, azimuths), jnp.float32)] * 2,
    )(turn_of, re, im)


def solution(mesh):
    in_specs = (
        P("az", None, None, "rng"),
        P(),
        P("rng", "az", None),
        P(None, "az", "rng", None),
        P(None, None, "az"),
    )
    out_specs = P("rng", None, "az")
    return jax.shard_map(
        per_device, mesh=mesh, in_specs=in_specs, out_specs=out_specs, check_vma=False
    )
```

```python
import functools

import jax
import jax.numpy as jnp
from jax import lax
from jax.experimental import pallas as pl
from jax.experimental.pallas import tpu as pltpu
from jax.sharding import PartitionSpec as P

GUARD = 128
MESH = pl.DeviceIdType.MESH
RIGHT, LEFT, SIBLING, LOW, HIGH = 0, 2, 4, 6, 7
HALVES = 2


def sine_cosine(x):
    turns = jnp.floor(x * 0.6366197723675814 + 0.5)
    r = x - turns * 1.5703125
    r = r - turns * 4.837512969970703e-4
    r = r - turns * 7.549789948768648e-8
    quadrant = turns.astype(jnp.int32)
    r2 = r * r
    s = r + r * r2 * (-1 / 6 + r2 * (1 / 120 + r2 * (-1 / 5040 + r2 * (1 / 362880))))
    c = 1.0 + r2 * (-0.5 + r2 * (1 / 24 + r2 * (-1 / 720 + r2 * (1 / 40320))))
    odd = (quadrant & 1) == 1
    sine = jnp.where(odd, c, s)
    cosine = jnp.where(odd, s, c)
    sine = jnp.where((quadrant & 2) == 2, -sine, sine)
    cosine = jnp.where(((quadrant + 1) & 2) == 2, -cosine, cosine)
    return sine, cosine


def transposed_dot(a, b):
    return lax.dot_general(a, b, (((1,), (1,)), ((), ())), preferred_element_type=jnp.float32)


def kernel(
    n_rng, n_az, pings, blocks,
    owner, start, echo, interp, phase,
    out_re, out_im, turn_of,
    window, interp_v, phase_v, shifted, steer, focus, image, column, sums, totals,
    load_sem, send_sem, recv_sem, column_sem, sum_send, sum_recv, total_send, total_recv,
):
    rng, az = lax.axis_index("rng"), lax.axis_index("az")
    chips = n_az // 2
    chip, core = az // 2, az % 2
    width = echo.shape[1]
    rows = echo.shape[0]
    half = rows // 2
    cells = interp.shape[1]
    band = interp.shape[2]
    azimuths = phase.shape[2]
    block = cells // blocks
    step = width // blocks
    scale = 1.0 / (pings * half) ** 0.5

    own_copy = pltpu.make_async_copy(echo, window.at[az, :, pl.ds(GUARD, width)], load_sem.at[0])
    own_copy.start()
    interp_copy = pltpu.make_async_copy(interp, interp_v, load_sem.at[1])
    interp_copy.start()
    phase_copy = pltpu.make_async_copy(phase, phase_v, load_sem.at[2])
    phase_copy.start()

    barrier = pltpu.get_barrier_semaphore()
    for turn in range(1, n_rng):
        pl.semaphore_signal(barrier, inc=1, device_id={"rng": lax.rem(rng + turn, n_rng)}, device_id_type=MESH)
    for turn in range(1, n_az):
        pl.semaphore_signal(barrier, inc=1, device_id={"az": lax.rem(az + turn, n_az)}, device_id_type=MESH)
    pl.semaphore_wait(barrier, n_rng + n_az - 2)

    def inner(slot):
        return window.at[slot, :, pl.ds(GUARD, width)]

    def push(src, dst, sent, got, target):
        return pltpu.make_async_remote_copy(
            src_ref=src, dst_ref=dst, send_sem=sent, recv_sem=got, device_id=target, device_id_type=MESH
        )

    def along(src, slot, kind, part):
        target = az + 1 - 2 * core if kind is SIBLING else az + 2 - 2 * kind
        lines = pl.ds(part * half, half)
        return push(
            src.at[lines, :], inner(slot).at[lines, :],
            send_sem.at[kind + part, slot], recv_sem.at[part, slot], {"az": target},
        )

    def edge_low(src, slot):
        return push(
            src.at[:, pl.ds(width - GUARD, GUARD)], window.at[slot, :, pl.ds(0, GUARD)],
            send_sem.at[LOW, slot], recv_sem.at[HALVES, slot], {"rng": rng + 1},
        )

    def edge_high(src, slot):
        return push(
            src.at[:, pl.ds(0, GUARD)], window.at[slot, :, pl.ds(GUARD + width, GUARD)],
            send_sem.at[HIGH, slot], recv_sem.at[HALVES + 1, slot], {"rng": rng - 1},
        )

    def send_edges(src, slot):
        @pl.when(rng + 1 < n_rng)
        def _():
            edge_low(src, slot).start()

        @pl.when(rng > 0)
        def _():
            edge_high(src, slot).start()

    def wait_edges(slot):
        @pl.when(rng > 0)
        def _():
            edge_low(inner(slot), slot).wait_recv()

        @pl.when(rng + 1 < n_rng)
        def _():
            edge_high(inner(slot), slot).wait_recv()

    def directions():
        for turn in range(2):
            sign = 1 - 2 * ((core + turn) % 2)
            onward = chip + sign
            yield sign, 1 - sign, (onward >= 0) & (onward < chips)

    def send_own(part):
        for _, kind, more in directions():
            @pl.when(more)
            def _():
                along(echo, az, kind, part).start()

    send_own(0)
    for part in range(HALVES):
        along(echo, az, SIBLING, part).start()
    send_edges(echo, az)
    send_own(1)

    @pl.when(rng == 0)
    def _():
        window[:, :, 0:GUARD] = jnp.zeros((n_az, rows, GUARD), window.dtype)

    @pl.when(rng == n_rng - 1)
    def _():
        window[:, :, GUARD + width:] = jnp.zeros((n_az, rows, GUARD), window.dtype)

    def prepare(where):
        for side in range(2):
            slot = 2 * where + side
            ping = jnp.int32(0)
            used = jnp.float32(0.0)
            for p in range(pings):
                hit = owner[p] == slot
                ping = jnp.where(hit, p, ping)
                used = jnp.where(hit, 1.0, used)

            def one_block(g, carry):
                part = interp_v[ping, pl.ds(g * block, block), :].astype(jnp.float32)
                if n_az != pings:
                    part = part * used
                move = start[g, 0, ping] - g * step
                lane = lax.broadcasted_iota(jnp.int32, (block, band), 1)
                part = pltpu.roll(part, lax.rem(move, band), 1)
                near = lane >= move
                shifted[slot, g, block:, :] = jnp.where(near, part, 0.0).astype(jnp.bfloat16)
                shifted[slot, g + 1, 0:block, :] = jnp.where(near, 0.0, part).astype(jnp.bfloat16)
                return carry

            lax.fori_loop(0, blocks, one_block, 0, unroll=2)

            def one_rows(k, carry):
                sine, cosine = sine_cosine(phase_v[ping, pl.ds(k * 16, 16), :])
                sine, cosine = sine * scale, cosine * scale
                top = pl.ds(side * rows + k * 16, 16)
                low = pl.ds(side * rows + half + k * 16, 16)
                steer[where, top, 0:azimuths] = cosine.astype(jnp.bfloat16)
                steer[where, top, azimuths:] = sine.astype(jnp.bfloat16)
                steer[where, low, 0:azimuths] = (-sine).astype(jnp.bfloat16)
                steer[where, low, azimuths:] = cosine.astype(jnp.bfloat16)
                return carry

            lax.fori_loop(0, half // 16, one_rows, 0)

    def compute(where, first):
        for side in range(2):
            slot = 2 * where + side
            columns = slice(side * rows, (side + 1) * rows)
            before = None
            for k in range(blocks + 1):
                low = block if k == 0 else 0
                high = block if k == blocks else 2 * block
                got = transposed_dot(shifted[slot, k, low:high, :], window[slot, :, k * step:(k + 1) * step])
                if k > 0:
                    focus[(k - 1) * block:k * block, columns] = (before + got[0:block]).astype(jnp.bfloat16)
                before = got[block - low:]

        def one_part(k, carry):
            columns = pl.ds(k * 256, 256)
            got = jnp.dot(focus[...], steer[where, :, columns], preferred_element_type=jnp.float32)
            if first:
                image[:, columns] = got
            else:
                image[:, columns] = image[:, columns] + got
            return carry

        lax.fori_loop(0, 2 * azimuths // 256, one_part, 0)

    def sides_at(distance):
        for sign, kind, more in directions():
            where = chip - sign * distance
            yield where, (where >= 0) & (where < chips), kind, more

    def forward(distance, part):
        for where, there, kind, more in sides_at(distance):
            @pl.when(there)
            def _():
                slot = 2 * where + core
                along(inner(slot), slot, kind, part).wait_recv()

                @pl.when(more)
                def _():
                    along(inner(slot), slot, kind, part).start()

                along(inner(slot), slot, SIBLING, part).start()
                if part == HALVES - 1:
                    send_edges(inner(slot), slot)

    def from_sibling(where):
        slot = 2 * where + 1 - core
        for part in range(HALVES):
            along(inner(slot), slot, SIBLING, part).wait_recv()
        send_edges(inner(slot), slot)

    def finish(where, first):
        wait_edges(2 * where)
        wait_edges(2 * where + 1)
        compute(where, first)

    interp_copy.wait()
    phase_copy.wait()
    prepare(chip)
    own_copy.wait()
    from_sibling(chip)
    finish(chip, True)
    between = (chip > 0) & (chip + 1 < chips)

    def at_distance(distance, carry):
        forward(distance, 0)
        early = (distance == 1) | jnp.logical_not(between)
        sides = [(where, there) for where, there, _, _ in sides_at(distance)]
        for where, there in sides:
            @pl.when(there & early)
            def _():
                prepare(where)

        forward(distance, 1)
        for where, there in sides:
            @pl.when(there & jnp.logical_not(early))
            def _():
                prepare(where)

        for where, there in sides:
            @pl.when(there)
            def _():
                from_sibling(where)

        for where, there in sides:
            @pl.when(there)
            def _():
                finish(where, False)

        return carry

    lax.fori_loop(1, chips, at_distance, 0)

    def one_group(k, carry):
        cross_re, cross_im, power = carry
        at = pl.ds(k * 16, 16)
        re16 = image[at, 0:azimuths].astype(jnp.bfloat16)
        im16 = image[at, azimuths:].astype(jnp.bfloat16)
        out_re[at, :] = re16
        out_im[at, :] = im16
        re, im = re16.astype(jnp.float32), im16.astype(jnp.float32)
        re_next = pltpu.roll(re, azimuths - 1, 1)
        im_next = pltpu.roll(im, azimuths - 1, 1)

        def fold(x):
            return x[0:8] + x[8:16]

        return (
            cross_re + fold(re * re_next + im * im_next),
            cross_im + fold(re * im_next - im * re_next),
            power + fold(re * re + im * im),
        )

    zero = jnp.zeros((8, azimuths), jnp.float32)
    cross_re, cross_im, power = lax.fori_loop(0, cells // 16, one_group, (zero, zero, zero), unroll=2)

    row16 = lax.broadcasted_iota(jnp.int32, (16, 128), 0)
    lane16 = lax.broadcasted_iota(jnp.int32, (16, 128), 1)

    def pick(row, lane):
        return jnp.where((row16 == row) & (lane16 == lane), 1.0, 0.0).astype(jnp.bfloat16)

    head = transposed_dot(pick(0, 0), out_re[:, 0:128]) + transposed_dot(pick(1, 0), out_im[:, 0:128])
    column[0] = head[0:8]
    send_column = push(
        column.at[0], column.at[1], column_sem.at[0], column_sem.at[1], {"az": lax.rem(az + n_az - 1, n_az)}
    )
    send_column.start()
    tail_re = transposed_dot(pick(0, 127), out_re[:, azimuths - 128:])
    tail_im = transposed_dot(pick(0, 127), out_im[:, azimuths - 128:])
    send_column.wait_recv()
    next_re, next_im = column[1, 0:1, :], column[1, 1:2, :]
    last_re, last_im = tail_re[0:1], tail_im[0:1]
    inside = jnp.where(az == n_az - 1, 0.0, 1.0)
    edge_re = jnp.sum(last_re * next_re + last_im * next_im, axis=1, keepdims=True) * inside
    edge_im = jnp.sum(last_re * next_im - last_im * next_re, axis=1, keepdims=True) * inside

    lane = lax.broadcasted_iota(jnp.int32, (8, azimuths), 1)
    row = lax.broadcasted_iota(jnp.int32, (8, azimuths), 0)
    at_end = lane == azimuths - 1
    cross_re = jnp.where(at_end, edge_re, jnp.sum(cross_re, axis=0, keepdims=True))
    cross_im = jnp.where(at_end, edge_im, jnp.sum(cross_im, axis=0, keepdims=True))
    power = jnp.sum(power, axis=0, keepdims=True)
    sums[rng] = jnp.where(row == 0, cross_re, jnp.where(row == 1, cross_im, power))

    def send_sums(turn):
        peer = lax.rem(rng + turn, n_rng)
        return push(sums.at[rng], sums.at[rng], sum_send.at[turn], sum_recv.at[rng], {"rng": peer})

    def take_sums(turn):
        peer = lax.rem(rng + turn, n_rng)
        return push(sums.at[peer], sums.at[peer], sum_send.at[turn], sum_recv.at[peer], {"rng": peer})

    for turn in range(1, n_rng):
        send_sums(turn).start()
    for turn in range(1, n_rng):
        take_sums(turn).wait_recv()
    total = sums[0]
    for turn in range(1, n_rng):
        total = total + sums[turn]
    cross_re, cross_im, power = total[0:1], total[1:2], total[2:3] + 1e-06
    slope = cross_im / power
    slope = slope + (cross_im * jnp.cos(slope) - cross_re * jnp.sin(slope)) / power
    slope = jnp.broadcast_to(slope, (8, azimuths))
    running = slope
    reach = 1
    while reach < azimuths:
        running = running + jnp.where(lane >= reach, pltpu.roll(running, reach, 1), 0.0)
        reach *= 2
    everything = jnp.sum(jnp.where(at_end, running, 0.0), axis=1, keepdims=True)
    totals[az] = jnp.broadcast_to(everything, (8, 128))

    def send_total(turn):
        peer = lax.rem(az + turn, n_az)
        return push(totals.at[az], totals.at[az], total_send.at[turn], total_recv.at[az], {"az": peer})

    def take_total(turn):
        peer = lax.rem(az + turn, n_az)
        return push(totals.at[peer], totals.at[peer], total_send.at[turn], total_recv.at[peer], {"az": peer})

    for turn in range(1, n_az):
        send_total(turn).start()
    for turn in range(1, n_az):
        take_total(turn).wait_recv()
    offset = jnp.zeros((8, 128), jnp.float32)
    for place in range(n_az):
        offset = offset + jnp.where(place < az, totals[place], 0.0)
    angle = offset[:, 0:1] + running - slope
    turn_of[0] = jnp.cos(angle)
    turn_of[1] = jnp.sin(angle)

    send_column.wait_send()
    for turn in range(1, n_rng):
        send_sums(turn).wait_send()
    for turn in range(1, n_az):
        send_total(turn).wait_send()

    def ended(slot, carry):
        where = slot // 2
        for part in range(HALVES):
            @pl.when(slot % 2 == core)
            def _():
                along(inner(slot), slot, SIBLING, part).wait_send()

                @pl.when((where <= chip) & (chip + 1 < chips))
                def _():
                    along(inner(slot), slot, RIGHT, part).wait_send()

                @pl.when((where >= chip) & (chip > 0))
                def _():
                    along(inner(slot), slot, LEFT, part).wait_send()

        @pl.when(rng + 1 < n_rng)
        def _():
            edge_low(inner(slot), slot).wait_send()

        @pl.when(rng > 0)
        def _():
            edge_high(inner(slot), slot).wait_send()

        return carry

    lax.fori_loop(0, n_az, ended, 0)


def turned(turn_of, in_re, in_im, out, mixed):
    lines, azimuths = in_re.shape
    tiles = azimuths // 128
    for t in range(tiles):
        lanes = slice(t * 128, (t + 1) * 128)
        cosine, sine = turn_of[0, 0:1, lanes], turn_of[1, 0:1, lanes]
        re, im = in_re[:, lanes].astype(jnp.float32), in_im[:, lanes].astype(jnp.float32)
        mixed[pl.ds(2 * t, lines, stride=2 * tiles), :] = re * cosine + im * sine
        mixed[pl.ds(2 * t + 1, lines, stride=2 * tiles), :] = im * cosine - re * sine
    out[...] = mixed[...].astype(jnp.bfloat16)


def per_device(echoes, owner_map, band_start, interp, steer_phase):
    n_rng, n_az = lax.axis_size("rng"), lax.axis_size("az")
    pings = owner_map.shape[0]
    blocks = band_start.shape[0]
    echo = echoes.reshape(echoes.shape[1] * echoes.shape[2], echoes.shape[3])
    interp = interp[:, 0]
    rows, width = echo.shape
    cells, band = interp.shape[1:]
    azimuths = steer_phase.shape[2]
    smem = pl.BlockSpec(memory_space=pltpu.SMEM)
    anywhere = pl.BlockSpec(memory_space=pl.ANY)
    vmem = pl.BlockSpec(memory_space=pltpu.VMEM)
    part = jax.ShapeDtypeStruct((cells, azimuths), jnp.bfloat16)
    dma = pltpu.SemaphoreType.DMA
    re, im, turn_of = pl.pallas_call(
        functools.partial(kernel, n_rng, n_az, pings, blocks),
        out_shape=(part, part, jax.ShapeDtypeStruct((2, 8, azimuths), jnp.float32)),
        in_specs=[smem, smem, anywhere, anywhere, anywhere],
        out_specs=(vmem, vmem, vmem),
        scratch_shapes=[
            pltpu.VMEM((n_az, rows, width + 2 * GUARD), jnp.bfloat16),
            pltpu.VMEM(interp.shape, jnp.bfloat16),
            pltpu.VMEM(steer_phase.shape, jnp.float32),
            pltpu.VMEM((n_az, blocks + 1, 2 * cells // blocks, band), jnp.bfloat16),
            pltpu.VMEM((n_az // 2, 2 * rows, 2 * azimuths), jnp.bfloat16),
            pltpu.VMEM((cells, 2 * rows), jnp.bfloat16),
            pltpu.VMEM((cells, 2 * azimuths), jnp.float32),
            pltpu.VMEM((2, 8, cells), jnp.float32),
            pltpu.VMEM((n_rng, 8, azimuths), jnp.float32),
            pltpu.VMEM((n_az, 8, 128), jnp.float32),
            dma((3,)), dma((3 * HALVES + 2, n_az)), dma((HALVES + 2, n_az)), dma((2,)),
            dma((n_rng,)), dma((n_rng,)), dma((n_az,)), dma((n_az,)),
        ],
        compiler_params=pltpu.CompilerParams(
            collective_id=0, has_side_effects=True, vmem_limit_bytes=56 * 1024 * 1024
        ),
    )(owner_map, band_start, echo, interp, steer_phase)
    lines = cells // 6
    tiles = azimuths // 128
    piece = pl.BlockSpec((lines, azimuths), lambda i: (i, 0))
    mixed = pl.pallas_call(
        turned,
        grid=(cells // lines,),
        out_shape=jax.ShapeDtypeStruct((cells * 2 * tiles, 128), jnp.bfloat16),
        in_specs=[pl.BlockSpec((2, 8, azimuths), lambda i: (0, 0, 0)), piece, piece],
        out_specs=pl.BlockSpec((lines * 2 * tiles, 128), lambda i: (i, 0)),
        scratch_shapes=[pltpu.VMEM((lines * 2 * tiles, 128), jnp.float32)],
    )(turn_of, re, im)
    mixed = mixed.reshape(cells, tiles, 2, 128)
    return jnp.transpose(mixed, (0, 2, 1, 3)).reshape(cells, 2, azimuths)


def solution(mesh):
    in_specs = (
        P("az", None, None, "rng"),
        P(),
        P("rng", "az", None),
        P(None, "az", "rng", None),
        P(None, None, "az"),
    )
    out_specs = P("rng", None, "az")
    return jax.shard_map(
        per_device, mesh=mesh, in_specs=in_specs, out_specs=out_specs, check_vma=False
    )
```

```python
import functools

import jax
import jax.numpy as jnp
from jax import lax
from jax.experimental import pallas as pl
from jax.experimental.pallas import tpu as pltpu
from jax.sharding import PartitionSpec as P

GUARD = 128
MESH = pl.DeviceIdType.MESH
RIGHT, LEFT, SIBLING, LOW, HIGH = 0, 2, 4, 6, 7
HALVES = 2


def sine_cosine(x):
    turns = jnp.floor(x * 0.6366197723675814 + 0.5)
    r = x - turns * 1.5703125
    r = r - turns * 4.837512969970703e-4
    r = r - turns * 7.549789948768648e-8
    quadrant = turns.astype(jnp.int32)
    r2 = r * r
    s = r + r * r2 * (-1 / 6 + r2 * (1 / 120 + r2 * (-1 / 5040 + r2 * (1 / 362880))))
    c = 1.0 + r2 * (-0.5 + r2 * (1 / 24 + r2 * (-1 / 720 + r2 * (1 / 40320))))
    odd = (quadrant & 1) == 1
    sine = jnp.where(odd, c, s)
    cosine = jnp.where(odd, s, c)
    sine = jnp.where((quadrant & 2) == 2, -sine, sine)
    cosine = jnp.where(((quadrant + 1) & 2) == 2, -cosine, cosine)
    return sine, cosine


def transposed_dot(a, b):
    return lax.dot_general(a, b, (((1,), (1,)), ((), ())), preferred_element_type=jnp.float32)


def kernel(
    n_rng, n_az, pings, blocks,
    owner, start, echo, interp, phase,
    given_re, given_im, turn_of,
    out_re, out_im,
    window, interp_v, phase_v, shifted, steer, focus, image, column, sums, totals,
    load_sem, send_sem, recv_sem, column_sem, sum_send, sum_recv, total_send, total_recv,
):
    rng, az = lax.axis_index("rng"), lax.axis_index("az")
    chips = n_az // 2
    chip, core = az // 2, az % 2
    width = echo.shape[1]
    rows = echo.shape[0]
    half = rows // 2
    cells = interp.shape[1]
    band = interp.shape[2]
    azimuths = phase.shape[2]
    block = cells // blocks
    step = width // blocks
    scale = 1.0 / (pings * half) ** 0.5

    own_copy = pltpu.make_async_copy(echo, window.at[az, :, pl.ds(GUARD, width)], load_sem.at[0])
    own_copy.start()
    interp_copy = pltpu.make_async_copy(interp, interp_v, load_sem.at[1])
    interp_copy.start()
    phase_copy = pltpu.make_async_copy(phase, phase_v, load_sem.at[2])
    phase_copy.start()

    barrier = pltpu.get_barrier_semaphore()
    for turn in range(1, n_rng):
        pl.semaphore_signal(barrier, inc=1, device_id={"rng": lax.rem(rng + turn, n_rng)}, device_id_type=MESH)
    for turn in range(1, n_az):
        pl.semaphore_signal(barrier, inc=1, device_id={"az": lax.rem(az + turn, n_az)}, device_id_type=MESH)
    pl.semaphore_wait(barrier, n_rng + n_az - 2)

    def inner(slot):
        return window.at[slot, :, pl.ds(GUARD, width)]

    def push(src, dst, sent, got, target):
        return pltpu.make_async_remote_copy(
            src_ref=src, dst_ref=dst, send_sem=sent, recv_sem=got, device_id=target, device_id_type=MESH
        )

    def along(src, slot, kind, part):
        target = az + 1 - 2 * core if kind is SIBLING else az + 2 - 2 * kind
        lines = pl.ds(part * half, half)
        return push(
            src.at[lines, :], inner(slot).at[lines, :],
            send_sem.at[kind + part, slot], recv_sem.at[part, slot], {"az": target},
        )

    def edge_low(src, slot):
        return push(
            src.at[:, pl.ds(width - GUARD, GUARD)], window.at[slot, :, pl.ds(0, GUARD)],
            send_sem.at[LOW, slot], recv_sem.at[HALVES, slot], {"rng": rng + 1},
        )

    def edge_high(src, slot):
        return push(
            src.at[:, pl.ds(0, GUARD)], window.at[slot, :, pl.ds(GUARD + width, GUARD)],
            send_sem.at[HIGH, slot], recv_sem.at[HALVES + 1, slot], {"rng": rng - 1},
        )

    def send_edges(src, slot):
        @pl.when(rng + 1 < n_rng)
        def _():
            edge_low(src, slot).start()

        @pl.when(rng > 0)
        def _():
            edge_high(src, slot).start()

    def wait_edges(slot):
        @pl.when(rng > 0)
        def _():
            edge_low(inner(slot), slot).wait_recv()

        @pl.when(rng + 1 < n_rng)
        def _():
            edge_high(inner(slot), slot).wait_recv()

    def directions():
        for turn in range(2):
            sign = 1 - 2 * ((core + turn) % 2)
            onward = chip + sign
            yield sign, 1 - sign, (onward >= 0) & (onward < chips)

    def send_own(part):
        for _, kind, more in directions():
            @pl.when(more)
            def _():
                along(echo, az, kind, part).start()

    send_own(0)
    for part in range(HALVES):
        along(echo, az, SIBLING, part).start()
    send_edges(echo, az)
    send_own(1)

    @pl.when(rng == 0)
    def _():
        window[:, :, 0:GUARD] = jnp.zeros((n_az, rows, GUARD), window.dtype)

    @pl.when(rng == n_rng - 1)
    def _():
        window[:, :, GUARD + width:] = jnp.zeros((n_az, rows, GUARD), window.dtype)

    def prepare(where):
        for side in range(2):
            slot = 2 * where + side
            ping = jnp.int32(0)
            used = jnp.float32(0.0)
            for p in range(pings):
                hit = owner[p] == slot
                ping = jnp.where(hit, p, ping)
                used = jnp.where(hit, 1.0, used)

            def one_block(g, carry):
                part = interp_v[ping, pl.ds(g * block, block), :].astype(jnp.float32)
                if n_az != pings:
                    part = part * used
                move = start[g, 0, ping] - g * step
                lane = lax.broadcasted_iota(jnp.int32, (block, band), 1)
                part = pltpu.roll(part, lax.rem(move, band), 1)
                near = lane >= move
                shifted[slot, g, block:, :] = jnp.where(near, part, 0.0).astype(jnp.bfloat16)
                shifted[slot, g + 1, 0:block, :] = jnp.where(near, 0.0, part).astype(jnp.bfloat16)
                return carry

            lax.fori_loop(0, blocks, one_block, 0, unroll=2)

            def one_rows(k, carry):
                sine, cosine = sine_cosine(phase_v[ping, pl.ds(k * 16, 16), :])
                sine, cosine = sine * scale, cosine * scale
                top = pl.ds(side * rows + k * 16, 16)
                low = pl.ds(side * rows + half + k * 16, 16)
                steer[where, top, 0:azimuths] = cosine.astype(jnp.bfloat16)
                steer[where, top, azimuths:] = sine.astype(jnp.bfloat16)
                steer[where, low, 0:azimuths] = (-sine).astype(jnp.bfloat16)
                steer[where, low, azimuths:] = cosine.astype(jnp.bfloat16)
                return carry

            lax.fori_loop(0, half // 16, one_rows, 0)

    def compute(where, first):
        for side in range(2):
            slot = 2 * where + side
            columns = slice(side * rows, (side + 1) * rows)
            before = None
            for k in range(blocks + 1):
                low = block if k == 0 else 0
                high = block if k == blocks else 2 * block
                got = transposed_dot(shifted[slot, k, low:high, :], window[slot, :, k * step:(k + 1) * step])
                if k > 0:
                    focus[(k - 1) * block:k * block, columns] = (before + got[0:block]).astype(jnp.bfloat16)
                before = got[block - low:]

        def one_part(k, carry):
            columns = pl.ds(k * 256, 256)
            got = jnp.dot(focus[...], steer[where, :, columns], preferred_element_type=jnp.float32)
            if first:
                image[:, columns] = got
            else:
                image[:, columns] = image[:, columns] + got
            return carry

        lax.fori_loop(0, 2 * azimuths // 256, one_part, 0)

    def sides_at(distance):
        for sign, kind, more in directions():
            where = chip - sign * distance
            yield where, (where >= 0) & (where < chips), kind, more

    def forward(distance, part):
        for where, there, kind, more in sides_at(distance):
            @pl.when(there)
            def _():
                slot = 2 * where + core
                along(inner(slot), slot, kind, part).wait_recv()

                @pl.when(more)
                def _():
                    along(inner(slot), slot, kind, part).start()

                along(inner(slot), slot, SIBLING, part).start()
                if part == HALVES - 1:
                    send_edges(inner(slot), slot)

    def from_sibling(where):
        slot = 2 * where + 1 - core
        for part in range(HALVES):
            along(inner(slot), slot, SIBLING, part).wait_recv()
        send_edges(inner(slot), slot)

    def finish(where, first):
        wait_edges(2 * where)
        wait_edges(2 * where + 1)
        compute(where, first)

    interp_copy.wait()
    phase_copy.wait()
    prepare(chip)
    own_copy.wait()
    from_sibling(chip)
    finish(chip, True)
    between = (chip > 0) & (chip + 1 < chips)

    def at_distance(distance, carry):
        early = (distance == 1) | jnp.logical_not(between)
        sides = [(where, there) for where, there, _, _ in sides_at(distance)]
        for where, there in sides:
            @pl.when(there & early)
            def _():
                prepare(where)

        forward(distance, 1)
        for where, there in sides:
            @pl.when(there & jnp.logical_not(early))
            def _():
                prepare(where)

        for where, there in sides:
            @pl.when(there)
            def _():
                from_sibling(where)

        (first, first_there), (second, second_there) = sides

        @pl.when(first_there)
        def _():
            finish(first, False)

        @pl.when(between)
        def _():
            forward(distance + 1, 0)

        @pl.when(second_there)
        def _():
            finish(second, False)

        @pl.when(jnp.logical_not(between))
        def _():
            forward(distance + 1, 0)

        return carry

    forward(1, 0)
    lax.fori_loop(1, chips, at_distance, 0)

    row16 = lax.broadcasted_iota(jnp.int32, (16, 128), 0)
    lane16 = lax.broadcasted_iota(jnp.int32, (16, 128), 1)

    def pick(row, lane):
        return jnp.where((row16 == row) & (lane16 == lane), 1.0, 0.0).astype(jnp.bfloat16)

    head = transposed_dot(pick(0, 0), image[:, 0:128].astype(jnp.bfloat16)) + transposed_dot(pick(1, 0), image[:, azimuths:azimuths + 128].astype(jnp.bfloat16))
    column[0] = head[0:8]
    send_column = push(
        column.at[0], column.at[1], column_sem.at[0], column_sem.at[1], {"az": lax.rem(az + n_az - 1, n_az)}
    )
    send_column.start()

    def one_group(k, carry):
        cross_re, cross_im, power = carry
        at = pl.ds(k * 16, 16)
        re16 = image[at, 0:azimuths].astype(jnp.bfloat16)
        im16 = image[at, azimuths:].astype(jnp.bfloat16)
        out_re[at, :] = re16
        out_im[at, :] = im16
        re, im = re16.astype(jnp.float32), im16.astype(jnp.float32)
        re_next = pltpu.roll(re, azimuths - 1, 1)
        im_next = pltpu.roll(im, azimuths - 1, 1)

        def fold(x):
            return x[0:8] + x[8:16]

        return (
            cross_re + fold(re * re_next + im * im_next),
            cross_im + fold(re * im_next - im * re_next),
            power + fold(re * re + im * im),
        )

    zero = jnp.zeros((8, azimuths), jnp.float32)
    cross_re, cross_im, power = lax.fori_loop(0, cells // 16, one_group, (zero, zero, zero), unroll=2)

    give_re = pltpu.make_async_copy(out_re, given_re, load_sem.at[0])
    give_im = pltpu.make_async_copy(out_im, given_im, load_sem.at[1])
    give_re.start()
    give_im.start()
    tail_re = transposed_dot(pick(0, 127), out_re[:, azimuths - 128:])
    tail_im = transposed_dot(pick(0, 127), out_im[:, azimuths - 128:])
    send_column.wait_recv()
    next_re, next_im = column[1, 0:1, :], column[1, 1:2, :]
    last_re, last_im = tail_re[0:1], tail_im[0:1]
    inside = jnp.where(az == n_az - 1, 0.0, 1.0)
    edge_re = jnp.sum(last_re * next_re + last_im * next_im, axis=1, keepdims=True) * inside
    edge_im = jnp.sum(last_re * next_im - last_im * next_re, axis=1, keepdims=True) * inside

    lane = lax.broadcasted_iota(jnp.int32, (8, azimuths), 1)
    row = lax.broadcasted_iota(jnp.int32, (8, azimuths), 0)
    at_end = lane == azimuths - 1
    cross_re = jnp.where(at_end, edge_re, jnp.sum(cross_re, axis=0, keepdims=True))
    cross_im = jnp.where(at_end, edge_im, jnp.sum(cross_im, axis=0, keepdims=True))
    power = jnp.sum(power, axis=0, keepdims=True)
    sums[rng] = jnp.where(row == 0, cross_re, jnp.where(row == 1, cross_im, power))

    def send_sums(turn):
        peer = lax.rem(rng + turn, n_rng)
        return push(sums.at[rng], sums.at[rng], sum_send.at[turn], sum_recv.at[rng], {"rng": peer})

    def take_sums(turn):
        peer = lax.rem(rng + turn, n_rng)
        return push(sums.at[peer], sums.at[peer], sum_send.at[turn], sum_recv.at[peer], {"rng": peer})

    for turn in range(1, n_rng):
        send_sums(turn).start()
    for turn in range(1, n_rng):
        take_sums(turn).wait_recv()
    total = sums[0]
    for turn in range(1, n_rng):
        total = total + sums[turn]
    cross_re, cross_im, power = total[0:1], total[1:2], total[2:3] + 1e-06
    slope = cross_im / power
    slope = slope + (cross_im * jnp.cos(slope) - cross_re * jnp.sin(slope)) / power
    slope = jnp.broadcast_to(slope, (8, azimuths))
    running = slope
    reach = 1
    while reach < azimuths:
        running = running + jnp.where(lane >= reach, pltpu.roll(running, reach, 1), 0.0)
        reach *= 2
    everything = jnp.sum(jnp.where(at_end, running, 0.0), axis=1, keepdims=True)
    totals[az] = jnp.broadcast_to(everything, (8, 128))

    def send_total(turn):
        peer = lax.rem(az + turn, n_az)
        return push(totals.at[az], totals.at[az], total_send.at[turn], total_recv.at[az], {"az": peer})

    def take_total(turn):
        peer = lax.rem(az + turn, n_az)
        return push(totals.at[peer], totals.at[peer], total_send.at[turn], total_recv.at[peer], {"az": peer})

    for turn in range(1, n_az):
        send_total(turn).start()
    for turn in range(1, n_az):
        take_total(turn).wait_recv()
    offset = jnp.zeros((8, 128), jnp.float32)
    for place in range(n_az):
        offset = offset + jnp.where(place < az, totals[place], 0.0)
    angle = offset[:, 0:1] + running - slope
    turn_of[0] = jnp.cos(angle)
    turn_of[1] = jnp.sin(angle)

    give_re.wait()
    give_im.wait()
    send_column.wait_send()
    for turn in range(1, n_rng):
        send_sums(turn).wait_send()
    for turn in range(1, n_az):
        send_total(turn).wait_send()

    def ended(slot, carry):
        where = slot // 2
        for part in range(HALVES):
            @pl.when(slot % 2 == core)
            def _():
                along(inner(slot), slot, SIBLING, part).wait_send()

                @pl.when((where <= chip) & (chip + 1 < chips))
                def _():
                    along(inner(slot), slot, RIGHT, part).wait_send()

                @pl.when((where >= chip) & (chip > 0))
                def _():
                    along(inner(slot), slot, LEFT, part).wait_send()

        @pl.when(rng + 1 < n_rng)
        def _():
            edge_low(inner(slot), slot).wait_send()

        @pl.when(rng > 0)
        def _():
            edge_high(inner(slot), slot).wait_send()

        return carry

    lax.fori_loop(0, n_az, ended, 0)


def turned(turn_of, in_re, in_im, out, mixed):
    lines, azimuths = in_re.shape
    tiles = azimuths // 128
    pitch = 2 * tiles + 1
    for t in range(tiles):
        lanes = slice(t * 128, (t + 1) * 128)
        cosine, sine = turn_of[0, 0:1, lanes], turn_of[1, 0:1, lanes]
        re, im = in_re[:, lanes].astype(jnp.float32), in_im[:, lanes].astype(jnp.float32)
        mixed[pl.ds(2 * t, lines, stride=pitch), :] = re * cosine + im * sine
        mixed[pl.ds(2 * t + 1, lines, stride=pitch), :] = im * cosine - re * sine
    for r in range(lines):
        out[r * 2 * tiles:(r + 1) * 2 * tiles, :] = mixed[r * pitch:r * pitch + 2 * tiles, :].astype(jnp.bfloat16)


def per_device(echoes, owner_map, band_start, interp, steer_phase):
    n_rng, n_az = lax.axis_size("rng"), lax.axis_size("az")
    pings = owner_map.shape[0]
    blocks = band_start.shape[0]
    echo = echoes.reshape(echoes.shape[1] * echoes.shape[2], echoes.shape[3])
    interp = interp[:, 0]
    rows, width = echo.shape
    cells, band = interp.shape[1:]
    azimuths = steer_phase.shape[2]
    smem = pl.BlockSpec(memory_space=pltpu.SMEM)
    anywhere = pl.BlockSpec(memory_space=pl.ANY)
    vmem = pl.BlockSpec(memory_space=pltpu.VMEM)
    part = jax.ShapeDtypeStruct((cells, azimuths), jnp.bfloat16)
    dma = pltpu.SemaphoreType.DMA
    re, im, turn_of = pl.pallas_call(
        functools.partial(kernel, n_rng, n_az, pings, blocks),
        out_shape=(part, part, jax.ShapeDtypeStruct((2, 8, azimuths), jnp.float32)),
        in_specs=[smem, smem, anywhere, anywhere, anywhere],
        out_specs=(anywhere, anywhere, vmem),
        scratch_shapes=[
            pltpu.VMEM((cells, azimuths), jnp.bfloat16),
            pltpu.VMEM((cells, azimuths), jnp.bfloat16),
            pltpu.VMEM((n_az, rows, width + 2 * GUARD), jnp.bfloat16),
            pltpu.VMEM(interp.shape, jnp.bfloat16),
            pltpu.VMEM(steer_phase.shape, jnp.float32),
            pltpu.VMEM((n_az, blocks + 1, 2 * cells // blocks, band), jnp.bfloat16),
            pltpu.VMEM((n_az // 2, 2 * rows, 2 * azimuths), jnp.bfloat16),
            pltpu.VMEM((cells, 2 * rows), jnp.bfloat16),
            pltpu.VMEM((cells, 2 * azimuths), jnp.float32),
            pltpu.VMEM((2, 8, cells), jnp.float32),
            pltpu.VMEM((n_rng, 8, azimuths), jnp.float32),
            pltpu.VMEM((n_az, 8, 128), jnp.float32),
            dma((3,)), dma((3 * HALVES + 2, n_az)), dma((HALVES + 2, n_az)), dma((2,)),
            dma((n_rng,)), dma((n_rng,)), dma((n_az,)), dma((n_az,)),
        ],
        compiler_params=pltpu.CompilerParams(
            collective_id=0, has_side_effects=True, vmem_limit_bytes=56 * 1024 * 1024
        ),
    )(owner_map, band_start, echo, interp, steer_phase)
    lines = cells // 6
    tiles = azimuths // 128
    piece = pl.BlockSpec((lines, azimuths), lambda i: (i, 0))
    mixed = pl.pallas_call(
        turned,
        grid=(cells // lines,),
        out_shape=jax.ShapeDtypeStruct((cells * 2 * tiles, 128), jnp.bfloat16),
        in_specs=[pl.BlockSpec((2, 8, azimuths), lambda i: (0, 0, 0)), piece, piece],
        out_specs=pl.BlockSpec((lines * 2 * tiles, 128), lambda i: (i, 0)),
        scratch_shapes=[pltpu.VMEM((lines * (2 * tiles + 1), 128), jnp.float32)],
    )(turn_of, re, im)
    mixed = mixed.reshape(cells, tiles, 2, 128)
    return jnp.transpose(mixed, (0, 2, 1, 3)).reshape(cells, 2, azimuths)


def solution(mesh):
    in_specs = (
        P("az", None, None, "rng"),
        P(),
        P("rng", "az", None),
        P(None, "az", "rng", None),
        P(None, None, "az"),
    )
    out_specs = P("rng", None, "az")
    return jax.shard_map(
        per_device, mesh=mesh, in_specs=in_specs, out_specs=out_specs, check_vma=False
    )
```

```python
import functools

import jax
import jax.numpy as jnp
from jax import lax
from jax.experimental import pallas as pl
from jax.experimental.pallas import tpu as pltpu
from jax.sharding import PartitionSpec as P

GUARD = 128
MESH = pl.DeviceIdType.MESH
RIGHT, LEFT, SIBLING, LOW, HIGH = 0, 2, 4, 6, 7
HALVES = 2


SINE = (
    1.0, -0.1666666716337204, 0.00833333283662796, -0.00019841254106722772, 2.7556704935705056e-06,
    -2.50387266476082e-08, 1.5896819971494835e-10, -6.611164523814828e-13,
)
COSINE = (
    1.0, -0.5, 0.0416666679084301, -0.00138888880610466, 2.4801563995424658e-05, -2.7556652071325516e-07,
    2.0865218441912248e-09, -1.1353691424520473e-11, 4.131706099214788e-14,
)


def series(terms, u):
    total = terms[-1] * u + terms[-2]
    for term in terms[-3::-1]:
        total = total * u + term
    return total


def sine_cosine(x):
    square = x * x
    return x * series(SINE, square), series(COSINE, square)


def transposed_dot(a, b):
    return lax.dot_general(a, b, (((1,), (1,)), ((), ())), preferred_element_type=jnp.float32)


def kernel(
    n_rng, n_az, pings, blocks,
    owner, start, echo, interp, phase,
    given_re, given_im, turn_of,
    out_re, out_im,
    window, interp_v, phase_v, shifted, steer, focus, image, column, sums, totals,
    load_sem, send_sem, recv_sem, column_sem, sum_send, sum_recv, total_send, total_recv,
):
    rng, az = lax.axis_index("rng"), lax.axis_index("az")
    chips = n_az // 2
    chip, core = az // 2, az % 2
    width = echo.shape[1]
    rows = echo.shape[0]
    half = rows // 2
    cells = interp.shape[1]
    band = interp.shape[2]
    azimuths = phase.shape[2]
    block = cells // blocks
    step = width // blocks
    scale = 1.0 / (pings * half) ** 0.5

    own_copy = pltpu.make_async_copy(echo, window.at[az, :, pl.ds(GUARD, width)], load_sem.at[0])
    own_copy.start()
    interp_copy = pltpu.make_async_copy(interp, interp_v, load_sem.at[1])
    interp_copy.start()
    phase_copy = pltpu.make_async_copy(phase, phase_v, load_sem.at[2])
    phase_copy.start()

    barrier = pltpu.get_barrier_semaphore()
    for turn in range(1, n_rng):
        pl.semaphore_signal(barrier, inc=1, device_id={"rng": lax.rem(rng + turn, n_rng)}, device_id_type=MESH)
    for turn in range(1, n_az):
        pl.semaphore_signal(barrier, inc=1, device_id={"az": lax.rem(az + turn, n_az)}, device_id_type=MESH)
    pl.semaphore_wait(barrier, n_rng + n_az - 2)

    def inner(slot):
        return window.at[slot, :, pl.ds(GUARD, width)]

    def push(src, dst, sent, got, target):
        return pltpu.make_async_remote_copy(
            src_ref=src, dst_ref=dst, send_sem=sent, recv_sem=got, device_id=target, device_id_type=MESH
        )

    def along(src, slot, kind, part):
        target = az + 1 - 2 * core if kind is SIBLING else az + 2 - 2 * kind
        lines = pl.ds(part * half, half)
        return push(
            src.at[lines, :], inner(slot).at[lines, :],
            send_sem.at[kind + part, slot], recv_sem.at[part, slot], {"az": target},
        )

    def edge_low(src, slot):
        return push(
            src.at[:, pl.ds(width - GUARD, GUARD)], window.at[slot, :, pl.ds(0, GUARD)],
            send_sem.at[LOW, slot], recv_sem.at[HALVES, slot], {"rng": rng + 1},
        )

    def edge_high(src, slot):
        return push(
            src.at[:, pl.ds(0, GUARD)], window.at[slot, :, pl.ds(GUARD + width, GUARD)],
            send_sem.at[HIGH, slot], recv_sem.at[HALVES + 1, slot], {"rng": rng - 1},
        )

    def send_edges(src, slot):
        @pl.when(rng + 1 < n_rng)
        def _():
            edge_low(src, slot).start()

        @pl.when(rng > 0)
        def _():
            edge_high(src, slot).start()

    def wait_edges(slot):
        @pl.when(rng > 0)
        def _():
            edge_low(inner(slot), slot).wait_recv()

        @pl.when(rng + 1 < n_rng)
        def _():
            edge_high(inner(slot), slot).wait_recv()

    def directions():
        for turn in range(2):
            sign = 1 - 2 * ((core + turn) % 2)
            onward = chip + sign
            yield sign, 1 - sign, (onward >= 0) & (onward < chips)

    def send_own(part):
        for _, kind, more in directions():
            @pl.when(more)
            def _():
                along(echo, az, kind, part).start()

    send_own(0)
    for part in range(HALVES):
        along(echo, az, SIBLING, part).start()
    send_edges(echo, az)
    send_own(1)

    @pl.when(rng == 0)
    def _():
        window[:, :, 0:GUARD] = jnp.zeros((n_az, rows, GUARD), window.dtype)

    @pl.when(rng == n_rng - 1)
    def _():
        window[:, :, GUARD + width:] = jnp.zeros((n_az, rows, GUARD), window.dtype)

    def prepare(where):
        for side in range(2):
            slot = 2 * where + side
            ping = jnp.int32(0)
            used = jnp.float32(0.0)
            for p in range(pings):
                hit = owner[p] == slot
                ping = jnp.where(hit, p, ping)
                used = jnp.where(hit, 1.0, used)

            def one_block(g, carry):
                part = interp_v[ping, pl.ds(g * block, block), :].astype(jnp.float32)
                if n_az != pings:
                    part = part * used
                move = start[g, 0, ping] - g * step
                lane = lax.broadcasted_iota(jnp.int32, (block, band), 1)
                part = pltpu.roll(part, lax.rem(move, band), 1)
                near = lane >= move
                shifted[slot, g, block:, :] = jnp.where(near, part, 0.0).astype(jnp.bfloat16)
                shifted[slot, g + 1, 0:block, :] = jnp.where(near, 0.0, part).astype(jnp.bfloat16)
                return carry

            lax.fori_loop(0, blocks, one_block, 0, unroll=2)

            def one_rows(k, carry):
                sine, cosine = sine_cosine(phase_v[ping, pl.ds(k * 16, 16), :])
                sine, cosine = sine * scale, cosine * scale
                top = pl.ds(side * rows + k * 16, 16)
                low = pl.ds(side * rows + half + k * 16, 16)
                steer[where, top, 0:azimuths] = cosine.astype(jnp.bfloat16)
                steer[where, top, azimuths:] = sine.astype(jnp.bfloat16)
                steer[where, low, 0:azimuths] = (-sine).astype(jnp.bfloat16)
                steer[where, low, azimuths:] = cosine.astype(jnp.bfloat16)
                return carry

            lax.fori_loop(0, half // 16, one_rows, 0)

    def compute(where, first):
        for side in range(2):
            slot = 2 * where + side
            columns = slice(side * rows, (side + 1) * rows)
            before = None
            for k in range(blocks + 1):
                low = block if k == 0 else 0
                high = block if k == blocks else 2 * block
                got = transposed_dot(shifted[slot, k, low:high, :], window[slot, :, k * step:(k + 1) * step])
                if k > 0:
                    focus[(k - 1) * block:k * block, columns] = (before + got[0:block]).astype(jnp.bfloat16)
                before = got[block - low:]

        def one_part(k, carry):
            columns = pl.ds(k * 256, 256)
            got = jnp.dot(focus[...], steer[where, :, columns], preferred_element_type=jnp.float32)
            if first:
                image[:, columns] = got
            else:
                image[:, columns] = image[:, columns] + got
            return carry

        lax.fori_loop(0, 2 * azimuths // 256, one_part, 0)

    def sides_at(distance):
        for sign, kind, more in directions():
            where = chip - sign * distance
            yield where, (where >= 0) & (where < chips), kind, more

    def forward(distance, part):
        for where, there, kind, more in sides_at(distance):
            @pl.when(there)
            def _():
                slot = 2 * where + core
                along(inner(slot), slot, kind, part).wait_recv()

                @pl.when(more)
                def _():
                    along(inner(slot), slot, kind, part).start()

                along(inner(slot), slot, SIBLING, part).start()
                if part == HALVES - 1:
                    send_edges(inner(slot), slot)

    def from_sibling(where):
        slot = 2 * where + 1 - core
        for part in range(HALVES):
            along(inner(slot), slot, SIBLING, part).wait_recv()
        send_edges(inner(slot), slot)

    def finish(where, first):
        wait_edges(2 * where)
        wait_edges(2 * where + 1)
        compute(where, first)

    interp_copy.wait()
    phase_copy.wait()
    prepare(chip)
    own_copy.wait()
    from_sibling(chip)
    forward(1, 0)
    finish(chip, True)
    between = (chip > 0) & (chip + 1 < chips)

    def at_distance(distance, carry):
        early = jnp.logical_not(between)
        sides = [(where, there) for where, there, _, _ in sides_at(distance)]
        for where, there in sides:
            @pl.when(there & early)
            def _():
                prepare(where)

        forward(distance, 1)
        for where, there in sides:
            @pl.when(there & jnp.logical_not(early))
            def _():
                prepare(where)

        for where, there in sides:
            @pl.when(there)
            def _():
                from_sibling(where)

        (first, first_there), (second, second_there) = sides

        @pl.when(first_there)
        def _():
            finish(first, False)

        @pl.when(between)
        def _():
            forward(distance + 1, 0)

        @pl.when(second_there)
        def _():
            finish(second, False)

        @pl.when(jnp.logical_not(between))
        def _():
            forward(distance + 1, 0)

        return carry

    lax.fori_loop(1, chips, at_distance, 0)

    row16 = lax.broadcasted_iota(jnp.int32, (16, 128), 0)
    lane16 = lax.broadcasted_iota(jnp.int32, (16, 128), 1)

    def pick(row, lane):
        return jnp.where((row16 == row) & (lane16 == lane), 1.0, 0.0).astype(jnp.bfloat16)

    head = transposed_dot(pick(0, 0), image[:, 0:128].astype(jnp.bfloat16)) + transposed_dot(pick(1, 0), image[:, azimuths:azimuths + 128].astype(jnp.bfloat16))
    column[0] = head[0:8]
    send_column = push(
        column.at[0], column.at[1], column_sem.at[0], column_sem.at[1], {"az": lax.rem(az + n_az - 1, n_az)}
    )
    send_column.start()

    def one_group(k, carry):
        cross_re, cross_im, power = carry
        at = pl.ds(k * 16, 16)
        re16 = image[at, 0:azimuths].astype(jnp.bfloat16)
        im16 = image[at, azimuths:].astype(jnp.bfloat16)
        out_re[at, :] = re16
        out_im[at, :] = im16
        re, im = re16.astype(jnp.float32), im16.astype(jnp.float32)
        re_next = pltpu.roll(re, azimuths - 1, 1)
        im_next = pltpu.roll(im, azimuths - 1, 1)

        def fold(x):
            return x[0:8] + x[8:16]

        return (
            cross_re + fold(re * re_next + im * im_next),
            cross_im + fold(re * im_next - im * re_next),
            power + fold(re * re + im * im),
        )

    zero = jnp.zeros((8, azimuths), jnp.float32)
    cross_re, cross_im, power = lax.fori_loop(0, cells // 16, one_group, (zero, zero, zero), unroll=2)

    give_re = pltpu.make_async_copy(out_re, given_re, load_sem.at[0])
    give_im = pltpu.make_async_copy(out_im, given_im, load_sem.at[1])
    give_re.start()
    give_im.start()
    tail_re = transposed_dot(pick(0, 127), out_re[:, azimuths - 128:])
    tail_im = transposed_dot(pick(0, 127), out_im[:, azimuths - 128:])
    send_column.wait_recv()
    next_re, next_im = column[1, 0:1, :], column[1, 1:2, :]
    last_re, last_im = tail_re[0:1], tail_im[0:1]
    inside = jnp.where(az == n_az - 1, 0.0, 1.0)
    edge_re = jnp.sum(last_re * next_re + last_im * next_im, axis=1, keepdims=True) * inside
    edge_im = jnp.sum(last_re * next_im - last_im * next_re, axis=1, keepdims=True) * inside

    lane = lax.broadcasted_iota(jnp.int32, (8, azimuths), 1)
    row = lax.broadcasted_iota(jnp.int32, (8, azimuths), 0)
    at_end = lane == azimuths - 1
    cross_re = jnp.where(at_end, edge_re, jnp.sum(cross_re, axis=0, keepdims=True))
    cross_im = jnp.where(at_end, edge_im, jnp.sum(cross_im, axis=0, keepdims=True))
    power = jnp.sum(power, axis=0, keepdims=True)
    sums[rng] = jnp.where(row == 0, cross_re, jnp.where(row == 1, cross_im, power))

    def send_sums(turn):
        peer = lax.rem(rng + turn, n_rng)
        return push(sums.at[rng], sums.at[rng], sum_send.at[turn], sum_recv.at[rng], {"rng": peer})

    def take_sums(turn):
        peer = lax.rem(rng + turn, n_rng)
        return push(sums.at[peer], sums.at[peer], sum_send.at[turn], sum_recv.at[peer], {"rng": peer})

    for turn in range(1, n_rng):
        send_sums(turn).start()
    for turn in range(1, n_rng):
        take_sums(turn).wait_recv()
    total = sums[0]
    for turn in range(1, n_rng):
        total = total + sums[turn]
    cross_re, cross_im, power = total[0:1], total[1:2], total[2:3] + 1e-06
    slope = cross_im / power
    slope = slope + (cross_im * jnp.cos(slope) - cross_re * jnp.sin(slope)) / power
    slope = jnp.broadcast_to(slope, (8, azimuths))
    running = slope
    reach = 1
    while reach < azimuths:
        running = running + jnp.where(lane >= reach, pltpu.roll(running, reach, 1), 0.0)
        reach *= 2
    everything = jnp.sum(jnp.where(at_end, running, 0.0), axis=1, keepdims=True)
    totals[az] = jnp.broadcast_to(everything, (8, 128))

    def send_total(turn):
        peer = lax.rem(az + turn, n_az)
        return push(totals.at[az], totals.at[az], total_send.at[turn], total_recv.at[az], {"az": peer})

    def take_total(turn):
        peer = lax.rem(az + turn, n_az)
        return push(totals.at[peer], totals.at[peer], total_send.at[turn], total_recv.at[peer], {"az": peer})

    for turn in range(1, n_az):
        send_total(turn).start()
    for turn in range(1, n_az):
        take_total(turn).wait_recv()
    offset = jnp.zeros((8, 128), jnp.float32)
    for place in range(n_az):
        offset = offset + jnp.where(place < az, totals[place], 0.0)
    angle = offset[:, 0:1] + running - slope
    turn_of[0] = jnp.cos(angle)
    turn_of[1] = jnp.sin(angle)

    give_re.wait()
    give_im.wait()
    send_column.wait_send()
    for turn in range(1, n_rng):
        send_sums(turn).wait_send()
    for turn in range(1, n_az):
        send_total(turn).wait_send()

    def ended(slot, carry):
        where = slot // 2
        for part in range(HALVES):
            @pl.when(slot % 2 == core)
            def _():
                along(inner(slot), slot, SIBLING, part).wait_send()

                @pl.when((where <= chip) & (chip + 1 < chips))
                def _():
                    along(inner(slot), slot, RIGHT, part).wait_send()

                @pl.when((where >= chip) & (chip > 0))
                def _():
                    along(inner(slot), slot, LEFT, part).wait_send()

        @pl.when(rng + 1 < n_rng)
        def _():
            edge_low(inner(slot), slot).wait_send()

        @pl.when(rng > 0)
        def _():
            edge_high(inner(slot), slot).wait_send()

        return carry

    lax.fori_loop(0, n_az, ended, 0)


def turned(turn_of, in_re, in_im, out, mixed):
    lines, azimuths = in_re.shape
    tiles = azimuths // 128
    pitch = 2 * tiles + 1
    for t in range(tiles):
        lanes = slice(t * 128, (t + 1) * 128)
        cosine, sine = turn_of[0, 0:1, lanes], turn_of[1, 0:1, lanes]
        re, im = in_re[:, lanes].astype(jnp.float32), in_im[:, lanes].astype(jnp.float32)
        mixed[pl.ds(2 * t, lines, stride=pitch), :] = re * cosine + im * sine
        mixed[pl.ds(2 * t + 1, lines, stride=pitch), :] = im * cosine - re * sine
    for r in range(lines):
        out[r * 2 * tiles:(r + 1) * 2 * tiles, :] = mixed[r * pitch:r * pitch + 2 * tiles, :].astype(jnp.bfloat16)


def per_device(echoes, owner_map, band_start, interp, steer_phase):
    n_rng, n_az = lax.axis_size("rng"), lax.axis_size("az")
    pings = owner_map.shape[0]
    blocks = band_start.shape[0]
    echo = echoes.reshape(echoes.shape[1] * echoes.shape[2], echoes.shape[3])
    interp = interp[:, 0]
    rows, width = echo.shape
    cells, band = interp.shape[1:]
    azimuths = steer_phase.shape[2]
    smem = pl.BlockSpec(memory_space=pltpu.SMEM)
    anywhere = pl.BlockSpec(memory_space=pl.ANY)
    vmem = pl.BlockSpec(memory_space=pltpu.VMEM)
    part = jax.ShapeDtypeStruct((cells, azimuths), jnp.bfloat16)
    dma = pltpu.SemaphoreType.DMA
    re, im, turn_of = pl.pallas_call(
        functools.partial(kernel, n_rng, n_az, pings, blocks),
        out_shape=(part, part, jax.ShapeDtypeStruct((2, 8, azimuths), jnp.float32)),
        in_specs=[smem, smem, anywhere, anywhere, anywhere],
        out_specs=(anywhere, anywhere, vmem),
        scratch_shapes=[
            pltpu.VMEM((cells, azimuths), jnp.bfloat16),
            pltpu.VMEM((cells, azimuths), jnp.bfloat16),
            pltpu.VMEM((n_az, rows, width + 2 * GUARD), jnp.bfloat16),
            pltpu.VMEM(interp.shape, jnp.bfloat16),
            pltpu.VMEM(steer_phase.shape, jnp.float32),
            pltpu.VMEM((n_az, blocks + 1, 2 * cells // blocks, band), jnp.bfloat16),
            pltpu.VMEM((n_az // 2, 2 * rows, 2 * azimuths), jnp.bfloat16),
            pltpu.VMEM((cells, 2 * rows), jnp.bfloat16),
            pltpu.VMEM((cells, 2 * azimuths), jnp.float32),
            pltpu.VMEM((2, 8, cells), jnp.float32),
            pltpu.VMEM((n_rng, 8, azimuths), jnp.float32),
            pltpu.VMEM((n_az, 8, 128), jnp.float32),
            dma((3,)), dma((3 * HALVES + 2, n_az)), dma((HALVES + 2, n_az)), dma((2,)),
            dma((n_rng,)), dma((n_rng,)), dma((n_az,)), dma((n_az,)),
        ],
        compiler_params=pltpu.CompilerParams(
            collective_id=0, has_side_effects=True, vmem_limit_bytes=56 * 1024 * 1024
        ),
    )(owner_map, band_start, echo, interp, steer_phase)
    lines = cells // 6
    tiles = azimuths // 128
    piece = pl.BlockSpec((lines, azimuths), lambda i: (i, 0))
    mixed = pl.pallas_call(
        turned,
        grid=(cells // lines,),
        out_shape=jax.ShapeDtypeStruct((cells * 2 * tiles, 128), jnp.bfloat16),
        in_specs=[pl.BlockSpec((2, 8, azimuths), lambda i: (0, 0, 0)), piece, piece],
        out_specs=pl.BlockSpec((lines * 2 * tiles, 128), lambda i: (i, 0)),
        scratch_shapes=[pltpu.VMEM((lines * (2 * tiles + 1), 128), jnp.float32)],
    )(turn_of, re, im)
    mixed = mixed.reshape(cells, tiles, 2, 128)
    return jnp.transpose(mixed, (0, 2, 1, 3)).reshape(cells, 2, azimuths)


def solution(mesh):
    in_specs = (
        P("az", None, None, "rng"),
        P(),
        P("rng", "az", None),
        P(None, "az", "rng", None),
        P(None, None, "az"),
    )
    out_specs = P("rng", None, "az")
    return jax.shard_map(
        per_device, mesh=mesh, in_specs=in_specs, out_specs=out_specs, check_vma=False
    )
```

```python
import functools

import jax
import jax.numpy as jnp
from jax import lax
from jax.experimental import pallas as pl
from jax.experimental.pallas import tpu as pltpu
from jax.sharding import PartitionSpec as P

GUARD = 128
MESH = pl.DeviceIdType.MESH
RIGHT, LEFT, SIBLING, LOW, HIGH = 0, 2, 4, 6, 7
HALVES = 2


SINE = (
    1.0, -0.1666666716337204, 0.00833333283662796, -0.00019841254106722772, 2.7556704935705056e-06,
    -2.50387266476082e-08, 1.5896819971494835e-10, -6.611164523814828e-13,
)
COSINE = (
    1.0, -0.5, 0.0416666679084301, -0.00138888880610466, 2.4801563995424658e-05, -2.7556652071325516e-07,
    2.0865218441912248e-09, -1.1353691424520473e-11, 4.131706099214788e-14,
)


def series(terms, u):
    total = terms[-1] * u + terms[-2]
    for term in terms[-3::-1]:
        total = total * u + term
    return total


def sine_cosine(x):
    square = x * x
    return x * series(SINE, square), series(COSINE, square)


def transposed_dot(a, b):
    return lax.dot_general(a, b, (((1,), (1,)), ((), ())), preferred_element_type=jnp.float32)


def kernel(
    n_rng, n_az, pings, blocks,
    owner, start, echo, interp, phase,
    given_re, given_im, turn_of,
    out_re, out_im,
    window, interp_v, phase_v, shifted, steer, focus, image, column, sums, totals,
    load_sem, send_sem, recv_sem, column_sem, sum_send, sum_recv, total_send, total_recv,
):
    rng, az = lax.axis_index("rng"), lax.axis_index("az")
    chips = n_az // 2
    chip, core = az // 2, az % 2
    width = echo.shape[1]
    rows = echo.shape[0]
    half = rows // 2
    cells = interp.shape[1]
    band = interp.shape[2]
    azimuths = phase.shape[2]
    block = cells // blocks
    step = width // blocks
    scale = 1.0 / (pings * half) ** 0.5

    own_copy = pltpu.make_async_copy(echo, window.at[az, :, pl.ds(GUARD, width)], load_sem.at[0])
    own_copy.start()
    interp_copy = pltpu.make_async_copy(interp, interp_v, load_sem.at[1])
    interp_copy.start()
    phase_copy = pltpu.make_async_copy(phase, phase_v, load_sem.at[2])
    phase_copy.start()

    barrier = pltpu.get_barrier_semaphore()
    for turn in range(1, n_rng):
        pl.semaphore_signal(barrier, inc=1, device_id={"rng": lax.rem(rng + turn, n_rng)}, device_id_type=MESH)
    for turn in range(1, n_az):
        pl.semaphore_signal(barrier, inc=1, device_id={"az": lax.rem(az + turn, n_az)}, device_id_type=MESH)
    pl.semaphore_wait(barrier, n_rng + n_az - 2)

    def inner(slot):
        return window.at[slot, :, pl.ds(GUARD, width)]

    def push(src, dst, sent, got, target):
        return pltpu.make_async_remote_copy(
            src_ref=src, dst_ref=dst, send_sem=sent, recv_sem=got, device_id=target, device_id_type=MESH
        )

    def along(src, slot, kind, part):
        target = az + 1 - 2 * core if kind is SIBLING else az + 2 - 2 * kind
        lines = pl.ds(part * half, half)
        return push(
            src.at[lines, :], inner(slot).at[lines, :],
            send_sem.at[kind + part, slot], recv_sem.at[part, slot], {"az": target},
        )

    def edge_low(src, slot):
        return push(
            src.at[:, pl.ds(width - GUARD, GUARD)], window.at[slot, :, pl.ds(0, GUARD)],
            send_sem.at[LOW, slot], recv_sem.at[HALVES, slot], {"rng": rng + 1},
        )

    def edge_high(src, slot):
        return push(
            src.at[:, pl.ds(0, GUARD)], window.at[slot, :, pl.ds(GUARD + width, GUARD)],
            send_sem.at[HIGH, slot], recv_sem.at[HALVES + 1, slot], {"rng": rng - 1},
        )

    def send_edges(src, slot):
        @pl.when(rng + 1 < n_rng)
        def _():
            edge_low(src, slot).start()

        @pl.when(rng > 0)
        def _():
            edge_high(src, slot).start()

    def wait_edges(slot):
        @pl.when(rng > 0)
        def _():
            edge_low(inner(slot), slot).wait_recv()

        @pl.when(rng + 1 < n_rng)
        def _():
            edge_high(inner(slot), slot).wait_recv()

    def directions():
        for turn in range(2):
            sign = 1 - 2 * ((core + turn) % 2)
            onward = chip + sign
            yield sign, 1 - sign, (onward >= 0) & (onward < chips)

    def send_own(part):
        for _, kind, more in directions():
            @pl.when(more)
            def _():
                along(echo, az, kind, part).start()

    send_own(0)
    for part in range(HALVES):
        along(echo, az, SIBLING, part).start()
    send_edges(echo, az)
    send_own(1)

    @pl.when(rng == 0)
    def _():
        window[:, :, 0:GUARD] = jnp.zeros((n_az, rows, GUARD), window.dtype)

    @pl.when(rng == n_rng - 1)
    def _():
        window[:, :, GUARD + width:] = jnp.zeros((n_az, rows, GUARD), window.dtype)

    def prepare(where):
        for side in range(2):
            slot = 2 * where + side
            ping = jnp.int32(0)
            used = jnp.float32(0.0)
            for p in range(pings):
                hit = owner[p] == slot
                ping = jnp.where(hit, p, ping)
                used = jnp.where(hit, 1.0, used)

            def one_block(g, carry):
                part = interp_v[ping, pl.ds(g * block, block), :].astype(jnp.float32)
                if n_az != pings:
                    part = part * used
                move = start[g, 0, ping] - g * step
                lane = lax.broadcasted_iota(jnp.int32, (block, band), 1)
                part = pltpu.roll(part, lax.rem(move, band), 1)
                near = lane >= move
                shifted[slot, g, block:, :] = jnp.where(near, part, 0.0).astype(jnp.bfloat16)
                shifted[slot, g + 1, 0:block, :] = jnp.where(near, 0.0, part).astype(jnp.bfloat16)
                return carry

            lax.fori_loop(0, blocks, one_block, 0, unroll=2)

            def one_rows(k, carry):
                sine, cosine = sine_cosine(phase_v[ping, pl.ds(k * 16, 16), :])
                sine, cosine = sine * scale, cosine * scale
                top = pl.ds(side * rows + k * 16, 16)
                low = pl.ds(side * rows + half + k * 16, 16)
                steer[where, top, 0:azimuths] = cosine.astype(jnp.bfloat16)
                steer[where, top, azimuths:] = sine.astype(jnp.bfloat16)
                steer[where, low, 0:azimuths] = (-sine).astype(jnp.bfloat16)
                steer[where, low, azimuths:] = cosine.astype(jnp.bfloat16)
                return carry

            lax.fori_loop(0, half // 16, one_rows, 0)

    def compute(where, first):
        for side in range(2):
            slot = 2 * where + side
            columns = slice(side * rows, (side + 1) * rows)
            before = None
            for k in range(blocks + 1):
                low = block if k == 0 else 0
                high = block if k == blocks else 2 * block
                got = transposed_dot(shifted[slot, k, low:high, :], window[slot, :, k * step:(k + 1) * step])
                if k > 0:
                    focus[(k - 1) * block:k * block, columns] = (before + got[0:block]).astype(jnp.bfloat16)
                before = got[block - low:]

        def one_part(k, carry):
            columns = pl.ds(k * 256, 256)
            got = jnp.dot(focus[...], steer[where, :, columns], preferred_element_type=jnp.float32)
            if first:
                image[:, columns] = got
            else:
                image[:, columns] = image[:, columns] + got
            return carry

        lax.fori_loop(0, 2 * azimuths // 256, one_part, 0)

    def sides_at(distance):
        for sign, kind, more in directions():
            where = chip - sign * distance
            yield where, (where >= 0) & (where < chips), kind, more

    def forward(distance, part):
        for where, there, kind, more in sides_at(distance):
            @pl.when(there)
            def _():
                slot = 2 * where + core
                along(inner(slot), slot, kind, part).wait_recv()

                @pl.when(more)
                def _():
                    along(inner(slot), slot, kind, part).start()

                along(inner(slot), slot, SIBLING, part).start()
                if part == HALVES - 1:
                    send_edges(inner(slot), slot)

    def from_sibling(where):
        slot = 2 * where + 1 - core
        for part in range(HALVES):
            along(inner(slot), slot, SIBLING, part).wait_recv()
        send_edges(inner(slot), slot)

    def finish(where, first):
        wait_edges(2 * where)
        wait_edges(2 * where + 1)
        compute(where, first)

    interp_copy.wait()
    phase_copy.wait()
    prepare(chip)
    own_copy.wait()
    from_sibling(chip)
    forward(1, 0)
    finish(chip, True)
    between = (chip > 0) & (chip + 1 < chips)

    def at_distance(distance, carry):
        early = jnp.logical_not(between)
        sides = [(where, there) for where, there, _, _ in sides_at(distance)]
        for where, there in sides:
            @pl.when(there & early)
            def _():
                prepare(where)

        forward(distance, 1)
        for where, there in sides:
            @pl.when(there & jnp.logical_not(early))
            def _():
                prepare(where)

        for where, there in sides:
            @pl.when(there)
            def _():
                from_sibling(where)

        (first, first_there), (second, second_there) = sides

        @pl.when(first_there)
        def _():
            finish(first, False)

        @pl.when(between)
        def _():
            forward(distance + 1, 0)

        @pl.when(second_there)
        def _():
            finish(second, False)

        @pl.when(jnp.logical_not(between))
        def _():
            forward(distance + 1, 0)

        return carry

    lax.fori_loop(1, chips, at_distance, 0)

    row16 = lax.broadcasted_iota(jnp.int32, (16, 128), 0)
    lane16 = lax.broadcasted_iota(jnp.int32, (16, 128), 1)

    def pick(row, lane):
        return jnp.where((row16 == row) & (lane16 == lane), 1.0, 0.0).astype(jnp.bfloat16)

    head = transposed_dot(pick(0, 0), image[:, 0:128].astype(jnp.bfloat16)) + transposed_dot(pick(1, 0), image[:, azimuths:azimuths + 128].astype(jnp.bfloat16))
    column[0] = head[0:8]
    send_column = push(
        column.at[0], column.at[1], column_sem.at[0], column_sem.at[1], {"az": lax.rem(az + n_az - 1, n_az)}
    )
    send_column.start()

    def one_group(k, carry):
        cross_re, cross_im, power = carry
        at = pl.ds(k * 16, 16)
        re16 = image[at, 0:azimuths].astype(jnp.bfloat16)
        im16 = image[at, azimuths:].astype(jnp.bfloat16)
        out_re[at, :] = re16
        out_im[at, :] = im16
        re, im = re16.astype(jnp.float32), im16.astype(jnp.float32)
        re_next = pltpu.roll(re, azimuths - 1, 1)
        im_next = pltpu.roll(im, azimuths - 1, 1)

        def fold(x):
            return x[0:8] + x[8:16]

        return (
            cross_re + fold(re * re_next + im * im_next),
            cross_im + fold(re * im_next - im * re_next),
            power + fold(re * re + im * im),
        )

    zero = jnp.zeros((8, azimuths), jnp.float32)
    cross_re, cross_im, power = lax.fori_loop(0, cells // 16, one_group, (zero, zero, zero), unroll=2)

    give_re = pltpu.make_async_copy(out_re, given_re, load_sem.at[0])
    give_im = pltpu.make_async_copy(out_im, given_im, load_sem.at[1])
    give_re.start()
    give_im.start()
    tail_re = transposed_dot(pick(0, 127), out_re[:, azimuths - 128:])
    tail_im = transposed_dot(pick(0, 127), out_im[:, azimuths - 128:])
    send_column.wait_recv()
    next_re, next_im = column[1, 0:1, :], column[1, 1:2, :]
    last_re, last_im = tail_re[0:1], tail_im[0:1]
    inside = jnp.where(az == n_az - 1, 0.0, 1.0)
    edge_re = jnp.sum(last_re * next_re + last_im * next_im, axis=1, keepdims=True) * inside
    edge_im = jnp.sum(last_re * next_im - last_im * next_re, axis=1, keepdims=True) * inside

    lane = lax.broadcasted_iota(jnp.int32, (8, azimuths), 1)
    row = lax.broadcasted_iota(jnp.int32, (8, azimuths), 0)
    at_end = lane == azimuths - 1
    cross_re = jnp.where(at_end, edge_re, jnp.sum(cross_re, axis=0, keepdims=True))
    cross_im = jnp.where(at_end, edge_im, jnp.sum(cross_im, axis=0, keepdims=True))
    power = jnp.sum(power, axis=0, keepdims=True)
    sums[rng] = jnp.where(row == 0, cross_re, jnp.where(row == 1, cross_im, power))

    def send_sums(turn):
        peer = lax.rem(rng + turn, n_rng)
        return push(sums.at[rng], sums.at[rng], sum_send.at[turn], sum_recv.at[rng], {"rng": peer})

    def take_sums(turn):
        peer = lax.rem(rng + turn, n_rng)
        return push(sums.at[peer], sums.at[peer], sum_send.at[turn], sum_recv.at[peer], {"rng": peer})

    for turn in range(1, n_rng):
        send_sums(turn).start()

    def ended(slot, carry):
        where = slot // 2
        for part in range(HALVES):
            @pl.when(slot % 2 == core)
            def _():
                along(inner(slot), slot, SIBLING, part).wait_send()

                @pl.when((where <= chip) & (chip + 1 < chips))
                def _():
                    along(inner(slot), slot, RIGHT, part).wait_send()

                @pl.when((where >= chip) & (chip > 0))
                def _():
                    along(inner(slot), slot, LEFT, part).wait_send()

        @pl.when(rng + 1 < n_rng)
        def _():
            edge_low(inner(slot), slot).wait_send()

        @pl.when(rng > 0)
        def _():
            edge_high(inner(slot), slot).wait_send()

        return carry

    lax.fori_loop(0, n_az, ended, 0)

    for turn in range(1, n_rng):
        take_sums(turn).wait_recv()
    total = sums[0]
    for turn in range(1, n_rng):
        total = total + sums[turn]
    cross_re, cross_im, power = total[0:1], total[1:2], total[2:3] + 1e-06
    slope = cross_im / power
    slope = slope + (cross_im * jnp.cos(slope) - cross_re * jnp.sin(slope)) / power
    slope = jnp.broadcast_to(slope, (8, azimuths))
    running = slope
    reach = 1
    while reach < azimuths:
        running = running + jnp.where(lane >= reach, pltpu.roll(running, reach, 1), 0.0)
        reach *= 2
    everything = jnp.sum(jnp.where(at_end, running, 0.0), axis=1, keepdims=True)
    totals[az] = jnp.broadcast_to(everything, (8, 128))

    def send_total(turn):
        peer = lax.rem(az + turn, n_az)
        return push(totals.at[az], totals.at[az], total_send.at[turn], total_recv.at[az], {"az": peer})

    def take_total(turn):
        peer = lax.rem(az + turn, n_az)
        return push(totals.at[peer], totals.at[peer], total_send.at[turn], total_recv.at[peer], {"az": peer})

    for turn in range(1, n_az):
        send_total(turn).start()
    angle = running - slope
    cosine, sine = jnp.cos(angle), jnp.sin(angle)
    for turn in range(1, n_az):
        take_total(turn).wait_recv()
    offset = jnp.zeros((8, 128), jnp.float32)
    for place in range(n_az):
        offset = offset + jnp.where(place < az, totals[place], 0.0)
    offset_cosine, offset_sine = jnp.cos(offset)[:, 0:1], jnp.sin(offset)[:, 0:1]
    turn_of[0] = cosine * offset_cosine - sine * offset_sine
    turn_of[1] = sine * offset_cosine + cosine * offset_sine

    give_re.wait()
    give_im.wait()
    send_column.wait_send()
    for turn in range(1, n_rng):
        send_sums(turn).wait_send()
    for turn in range(1, n_az):
        send_total(turn).wait_send()


def turned(turn_of, in_re, in_im, out, mixed):
    lines, azimuths = in_re.shape
    tiles = azimuths // 128
    pitch = 2 * tiles + 1
    for t in range(tiles):
        lanes = slice(t * 128, (t + 1) * 128)
        cosine, sine = turn_of[0, 0:1, lanes], turn_of[1, 0:1, lanes]
        re, im = in_re[:, lanes].astype(jnp.float32), in_im[:, lanes].astype(jnp.float32)
        mixed[pl.ds(2 * t, lines, stride=pitch), :] = re * cosine + im * sine
        mixed[pl.ds(2 * t + 1, lines, stride=pitch), :] = im * cosine - re * sine
    for r in range(lines):
        out[r * 2 * tiles:(r + 1) * 2 * tiles, :] = mixed[r * pitch:r * pitch + 2 * tiles, :].astype(jnp.bfloat16)


def per_device(echoes, owner_map, band_start, interp, steer_phase):
    n_rng, n_az = lax.axis_size("rng"), lax.axis_size("az")
    pings = owner_map.shape[0]
    blocks = band_start.shape[0]
    echo = echoes.reshape(echoes.shape[1] * echoes.shape[2], echoes.shape[3])
    interp = interp[:, 0]
    rows, width = echo.shape
    cells, band = interp.shape[1:]
    azimuths = steer_phase.shape[2]
    smem = pl.BlockSpec(memory_space=pltpu.SMEM)
    anywhere = pl.BlockSpec(memory_space=pl.ANY)
    vmem = pl.BlockSpec(memory_space=pltpu.VMEM)
    part = jax.ShapeDtypeStruct((cells, azimuths), jnp.bfloat16)
    dma = pltpu.SemaphoreType.DMA
    re, im, turn_of = pl.pallas_call(
        functools.partial(kernel, n_rng, n_az, pings, blocks),
        out_shape=(part, part, jax.ShapeDtypeStruct((2, 8, azimuths), jnp.float32)),
        in_specs=[smem, smem, anywhere, anywhere, anywhere],
        out_specs=(anywhere, anywhere, vmem),
        scratch_shapes=[
            pltpu.VMEM((cells, azimuths), jnp.bfloat16),
            pltpu.VMEM((cells, azimuths), jnp.bfloat16),
            pltpu.VMEM((n_az, rows, width + 2 * GUARD), jnp.bfloat16),
            pltpu.VMEM(interp.shape, jnp.bfloat16),
            pltpu.VMEM(steer_phase.shape, jnp.float32),
            pltpu.VMEM((n_az, blocks + 1, 2 * cells // blocks, band), jnp.bfloat16),
            pltpu.VMEM((n_az // 2, 2 * rows, 2 * azimuths), jnp.bfloat16),
            pltpu.VMEM((cells, 2 * rows), jnp.bfloat16),
            pltpu.VMEM((cells, 2 * azimuths), jnp.float32),
            pltpu.VMEM((2, 8, cells), jnp.float32),
            pltpu.VMEM((n_rng, 8, azimuths), jnp.float32),
            pltpu.VMEM((n_az, 8, 128), jnp.float32),
            dma((3,)), dma((3 * HALVES + 2, n_az)), dma((HALVES + 2, n_az)), dma((2,)),
            dma((n_rng,)), dma((n_rng,)), dma((n_az,)), dma((n_az,)),
        ],
        compiler_params=pltpu.CompilerParams(
            collective_id=0, has_side_effects=True, vmem_limit_bytes=56 * 1024 * 1024
        ),
    )(owner_map, band_start, echo, interp, steer_phase)
    lines = cells // 6
    tiles = azimuths // 128
    piece = pl.BlockSpec((lines, azimuths), lambda i: (i, 0))
    mixed = pl.pallas_call(
        turned,
        grid=(cells // lines,),
        out_shape=jax.ShapeDtypeStruct((cells * 2 * tiles, 128), jnp.bfloat16),
        in_specs=[pl.BlockSpec((2, 8, azimuths), lambda i: (0, 0, 0)), piece, piece],
        out_specs=pl.BlockSpec((lines * 2 * tiles, 128), lambda i: (i, 0)),
        scratch_shapes=[pltpu.VMEM((lines * (2 * tiles + 1), 128), jnp.float32)],
    )(turn_of, re, im)
    mixed = mixed.reshape(cells, tiles, 2, 128)
    return jnp.transpose(mixed, (0, 2, 1, 3)).reshape(cells, 2, azimuths)


def solution(mesh):
    in_specs = (
        P("az", None, None, "rng"),
        P(),
        P("rng", "az", None),
        P(None, "az", "rng", None),
        P(None, None, "az"),
    )
    out_specs = P("rng", None, "az")
    return jax.shard_map(
        per_device, mesh=mesh, in_specs=in_specs, out_specs=out_specs, check_vma=False
    )
```
